512 devices in a mesh: gx: 32 (over x, y), gy: 16 (over z, core).
Axes of the slice: x: 4, y: 8, z: 8, core: 2. Of those that a mesh axis runs over, the one named last changes fastest.
Arguments:
- u_star: float32 [2, 1, 1536, 4096], P(None, None, 'gy', 'gx'), may hold values from -6 to 6
- v_star: float32 [2, 1, 1536, 4096], P(None, None, 'gy', 'gx'), may hold values from -6 to 6
- w_star: float32 [2, 1, 1536, 4096], P(None, None, 'gy', 'gx'), may hold values from -6 to 6
- cell_width: float32 [1536], P('gy'), may hold values from 0.0003841146 to 0.0055403646
- face_weight: float32 [1536], P('gy'), may hold values from 179.712 to 2560.512
Outputs:
- u_new: float32 [2, 1, 1536, 4096], P(None, None, 'gy', 'gx')
- v_new: float32 [2, 1, 1536, 4096], P(None, None, 'gy', 'gx')
- w_new: float32 [2, 1, 1536, 4096], P(None, None, 'gy', 'gx')
The draws below stay inside these ranges and needn't reach their ends.
All inputs are finite; a program needn't handle non-finite values.
Results may differ from the reference program's by a relative error of at most 0.0012.
Values sent between devices are 32-bit elements; how exact they have to be, the bound alone decides.
No kernel may reach another device: no remote copies, remote signals or barrier semaphores. Data moves between devices by JAX's collectives and lax.ppermute only.
A program may use at most 64 MiB of HBM per device.

```python
import jax
import jax.numpy as jnp
from jax import lax

K = 1
NX = 4096
NY = 1536


def grid_widths(key):
    index_vals = jnp.arange(NY, dtype=jnp.float32)
    shape_part = 0.3 + 1.4 * jnp.sin(jnp.pi * (index_vals + 0.5) / NY) ** 2
    rough_part = jnp.exp(jax.random.uniform(key, (NY,), jnp.float32) * jnp.log(2.5))
    return 2.0 / NY * shape_part * rough_part


def draw_cell_width(key, part):
    return grid_widths(key)


def draw_face_weight(key, part):
    widths = grid_widths(key)
    return 2.0 / (widths + jnp.roll(widths, -1))


def shard_levels(key, shape, shards, smallest, high):
    factor_of = 1.0
    for dim, shards_of in shards:
        steps = jax.random.uniform(jax.random.fold_in(jax.random.fold_in(key, 6), dim), (shards_of,), jnp.float32, smallest / len(shards), high / len(shards))
        factor_of = factor_of * jnp.repeat(jnp.exp(steps), shape[dim] // shards_of).reshape((-1,) + (1,) * (len(shape) - 1 - dim))
    return factor_of


def noise(own_key, shape, width, reach, split=(), held_as=jnp.bfloat16):
    values = jax.random.normal(own_key, shape, jnp.float32) * width
    if len(split) > 0:
        values = shard_levels(own_key, shape, split, -0.22, 0.18) * values
    return jnp.clip(values, min=-reach, max=reach).astype(held_as)


def setup_inputs(seed: int = 0) -> dict:
    arg_keys = jax.random.split(jax.random.key(seed), 6)
    return {
        "u_star": noise(arg_keys[0], (2, K, NY, NX), 1.0, 6.0, ((2, 16), (3, 32)), jnp.float32),
        "v_star": noise(arg_keys[1], (2, K, NY, NX), 1.0, 6.0, ((2, 16), (3, 32)), jnp.float32),
        "w_star": noise(arg_keys[2], (2, K, NY, NX), 1.0, 6.0, ((2, 16), (3, 32)), jnp.float32),
        "cell_width": draw_cell_width(jax.random.fold_in(arg_keys[5], 71), 0),
        "face_weight": draw_face_weight(jax.random.fold_in(arg_keys[5], 71), 0),
    }


FLOW_FACTOR = 0.5
SPAN_FACTOR = 1.0


def tridiagonal(diagonal, below_g, above_g, right_side):
    def downward(state_in, row_items):
        prev_c, prev_d = state_in
        diag_row, below_row, above_row, right_row = row_items
        pivot_val = diag_row + below_row * prev_c
        new_c = -above_row / pivot_val
        new_d = (right_row + below_row * prev_d) / pivot_val
        return (new_c, new_d), (new_c, new_d)

    zero_state = (jnp.zeros_like(diagonal[0]), jnp.zeros_like(right_side[0]))
    ignored, (upper_c, upper_d) = lax.scan(downward, zero_state, (diagonal, below_g, above_g, right_side))

    def upward(state_in, row_items):
        row_c, row_d = row_items
        solved_val = row_d - row_c * state_in
        return solved_val, solved_val

    ignored_last, solved = lax.scan(upward, jnp.zeros_like(right_side[0]), (upper_c, upper_d), reverse=True)
    return solved


def to_physical(field_pair):
    inverse_vals = jnp.fft.ifft(lax.complex(field_pair[0], field_pair[1]), axis=-1)
    return jnp.stack([jnp.real(inverse_vals), jnp.imag(inverse_vals)])


def reference(u_star, v_star, w_star, cell_width, face_weight):
    span_wave = ((jnp.arange(K) + 1) * SPAN_FACTOR).astype(jnp.float32)
    span_col = span_wave[:, None, None]
    wave_idx = jnp.arange(NX)
    signed = jnp.where(wave_idx < NX // 2, wave_idx, wave_idx - NX)
    flow_wave = signed.astype(jnp.float32) * FLOW_FACTOR
    g_masked = jnp.where(jnp.arange(NY) == NY - 1, jnp.zeros_like(face_weight), face_weight)
    g_below = jnp.concatenate([jnp.zeros_like(g_masked[:1]), g_masked[:-1]])
    width_col = cell_width[None, :, None]
    v_prev = jnp.concatenate([jnp.zeros_like(v_star[:, :, :1]), v_star[:, :, :-1]], axis=2)
    div_real = (v_star[0] - v_prev[0]) / width_col - span_col * w_star[1]
    div_imag = (v_star[1] - v_prev[1]) / width_col + span_col * w_star[0]
    u_hat = jnp.fft.fft(lax.complex(u_star[0], u_star[1]), axis=-1)
    div_hat = jnp.fft.fft(lax.complex(div_real, div_imag), axis=-1)
    rhs_real = jnp.real(div_hat) - flow_wave * jnp.imag(u_hat)
    rhs_imag = jnp.imag(div_hat) + flow_wave * jnp.real(u_hat)
    right_side = -width_col * jnp.stack([rhs_real, rhs_imag])
    right_rows = jnp.moveaxis(right_side, 2, 0)
    wave_sq = flow_wave[None, :] ** 2 + span_wave[:, None] ** 2
    diagonal = (g_masked + g_below)[:, None, None] + wave_sq[None] * cell_width[:, None, None]
    potential = jnp.moveaxis(tridiagonal(diagonal, g_below, g_masked, right_rows), 0, 2)
    pot_next = jnp.concatenate([potential[:, :, 1:], jnp.zeros_like(potential[:, :, :1])], axis=2)
    grad_y = g_masked[None, None, :, None] * (pot_next - potential)
    grad_x = jnp.stack([-flow_wave * potential[1], flow_wave * potential[0]])
    grad_z = jnp.stack([-span_col * potential[1], span_col * potential[0]])
    u_new = u_star - to_physical(grad_x)
    v_new = v_star - to_physical(grad_y)
    w_new = w_star - to_physical(grad_z)
    return (u_new, v_new, w_new)
```

```python
import functools
import math

import jax
import jax.numpy as jnp
import numpy as np
from jax import lax
from jax.experimental import pallas as pl
from jax.experimental.pallas import tpu as pltpu
from jax.sharding import PartitionSpec as P

FLOW_FACTOR = 0.5
SPAN_FACTOR = 1.0
KZ = SPAN_FACTOR
STANDIN = 16.0
HIGHEST = lax.Precision.HIGHEST
F32 = jnp.float32
VMEM = pl.BlockSpec(memory_space=pltpu.VMEM)
SEND_A, SEND_B, SEND_C, SEND_D = 16, 8, 8, 16


def tables(nodes, cols):
    full = nodes * cols

    def cos_sin(a, b, length):
        angle = 2.0 * np.pi * (np.outer(np.arange(a), np.arange(b)) % length) / length
        return np.cos(angle), np.sin(angle)

    c, s = cos_sin(nodes, nodes, nodes)
    across_f = np.block([[c, s], [-s, c]])
    across_i = np.block([[c, -s], [s, c]])
    c, s = cos_sin(cols, cols, cols)
    along_f = np.block([[c, -s], [s, c]])
    along_i = np.block([[c, s], [-s, c]]) / full
    turn = np.stack(cos_sin(nodes, cols, full))
    return [np.asarray(m, np.float32) for m in (across_f, across_i, along_f, along_i, turn)]


def dot(a, b):
    return lax.dot_general(a, b, (((1,), (0,)), ((), ())), precision=HIGHEST, preferred_element_type=F32)


def signed_half(wave, full):
    return jnp.where(wave < full // 2, wave, wave - full).astype(F32) * FLOW_FACTOR


def wavenumbers(nodes, cols):
    rank = lax.broadcasted_iota(jnp.int32, (nodes, cols), 0)
    place = lax.broadcasted_iota(jnp.int32, (nodes, cols), 1)
    return signed_half(rank + nodes * place, nodes * cols)


def column(row, rows, cols):
    here = lax.broadcasted_iota(jnp.int32, (rows, rows), 0)
    there = lax.broadcasted_iota(jnp.int32, (rows, rows), 1)
    one = jnp.sum(jnp.where(here == there, jnp.broadcast_to(row, (rows, rows)), 0.0), axis=1, keepdims=True)
    return jnp.broadcast_to(one, (rows, cols))


def prepare(nodes, u, v, w, width, weight, send, wide, heavy, tmp):
    rows, cols = u.shape[1:]
    per = rows // nodes
    h = column(width[...], rows, cols)
    wide[...] = h
    heavy[...] = column(weight[...], rows, cols)
    first = lax.broadcasted_iota(jnp.int32, (rows, cols), 0) == 0
    for part in range(2):
        tmp[part] = -h * u[part]
        now = v[part]
        below = jnp.where(first, 0.0, pltpu.roll(now, 1, 0))
        other = w[1 - part] * (h * KZ)
        tmp[2 + part] = below - now + (other if part == 0 else -other)
    for field in range(4):
        for t in range(per):
            send[pl.ds(field * per + t, nodes, stride=SEND_A), :] = tmp[field, pl.ds(t * nodes, nodes), :]
    for part in range(2):
        last = jnp.broadcast_to(v[part, rows - 1 : rows, :], (nodes, cols))
        send[pl.ds(4 * per + part, nodes, stride=SEND_A), :] = last
        send[pl.ds(4 * per + 2 + part, nodes, stride=SEND_A), :] = jnp.zeros_like(last)


def forward(nodes, per, got, across, along, turn, send, edge, pick):
    cols = got.shape[1]
    rank = lax.axis_index("gx")

    def slot(s):
        return got[pl.ds(s, nodes, stride=SEND_A), :]

    real = [slot(t) for t in range(per)] + [slot(2 * per + t) for t in range(per)] + [slot(4 * per)]
    imag = [slot(per + t) for t in range(per)] + [slot(3 * per + t) for t in range(per)] + [slot(4 * per + 1)]
    both = jnp.concatenate([jnp.concatenate(real, 1), jnp.concatenate(imag, 1)], 0)
    mixed = dot(across[...], both)
    c, s = turn[0], turn[1]
    turned = []
    for i in range(2 * per + 1):
        a = mixed[:nodes, i * cols : (i + 1) * cols]
        b = mixed[nodes:, i * cols : (i + 1) * cols]
        turned.append(jnp.concatenate([a * c + b * s, b * c - a * s], 1))
    pick[...] = turned[-1]
    mine = jnp.broadcast_to(pick[pl.ds(rank, 1), :], (8, 2 * cols))
    spectrum = dot(jnp.concatenate(turned[:-1] + [mine], 0), along[...])
    kx = wavenumbers(nodes, cols)
    for t in range(per):
        u = spectrum[t * nodes : (t + 1) * nodes]
        g = spectrum[(per + t) * nodes : (per + t + 1) * nodes]
        send[pl.ds(t, nodes, stride=SEND_B), :] = g[:, :cols] - kx * u[:, cols:]
        send[pl.ds(per + t, nodes, stride=SEND_B), :] = g[:, cols:] + kx * u[:, :cols]
    for part in range(2):
        send[pl.ds(2 * per + part, nodes, stride=SEND_B), :] = jnp.zeros((nodes, cols), F32)
        edge[part : part + 1, :] = spectrum[2 * per * nodes : 2 * per * nodes + 1, part * cols : (part + 1) * cols]


def eliminate(nodes, per, got, edge, wide, heavy, base, left, right, send, rhs, ratio):
    rows, cols = wide.shape
    steps = lax.axis_size("gy")
    rank_x, rank_y = lax.axis_index("gx"), lax.axis_index("gy")
    for part in range(2):
        for t in range(per):
            rhs[part, pl.ds(t * nodes, nodes), :] = got[pl.ds(part * per + t, nodes, stride=SEND_B), :]
    place = lax.broadcasted_iota(jnp.int32, (1, cols), 1)
    kx = signed_half(rank_x + nodes * place, nodes * cols)
    square = kx * kx + KZ * KZ
    top = heavy[rows - 1 : rows, :]
    above_last = jnp.where(rank_y == steps - 1, 0.0, top)
    below_first = jnp.where(rank_y == 0, 0.0, jnp.full((1, cols), STANDIN, F32))

    def above(j):
        return above_last if j == rows - 1 else heavy[j : j + 1, :]

    def below(j):
        return below_first if j == 0 else heavy[j - 1 : j, :]

    def diagonal(j):
        return above(j) + below(j) + square * wide[j : j + 1, :]

    half = rows // 2
    low = high = None
    for i in range(half):
        j, k = i, rows - 1 - i
        if i == 0:
            inv_l, inv_h = 1.0 / diagonal(j), 1.0 / diagonal(k)
            low = (rhs[0, j : j + 1, :] * inv_l, rhs[1, j : j + 1, :] * inv_l, inv_l)
            high = (rhs[0, k : k + 1, :] * inv_h, rhs[1, k : k + 1, :] * inv_h, inv_h)
        else:
            gl, gh = below(j), above(k)
            inv_l = 1.0 / (diagonal(j) - gl * gl * inv_l)
            inv_h = 1.0 / (diagonal(k) - gh * gh * inv_h)
            low = (
                (rhs[0, j : j + 1, :] + gl * low[0]) * inv_l,
                (rhs[1, j : j + 1, :] + gl * low[1]) * inv_l,
                gl * low[2] * inv_l,
            )
            high = (
                (rhs[0, k : k + 1, :] + gh * high[0]) * inv_h,
                (rhs[1, k : k + 1, :] + gh * high[1]) * inv_h,
                gh * high[2] * inv_h,
            )
        e_l, e_h = above(j) * inv_l, below(k) * inv_h
        if i < half - 1:
            ratio[j : j + 1, :] = e_l
            ratio[k : k + 1, :] = e_h
            for part in range(2):
                base[part, j : j + 1, :] = low[part]
                base[part, k : k + 1, :] = high[part]
            left[j : j + 1, :] = low[2]
            right[k : k + 1, :] = high[2]
    meet = 1.0 / (1.0 - e_l * e_h)
    down = [(low[0] + e_l * high[0]) * meet, (low[1] + e_l * high[1]) * meet, low[2] * meet, e_l * high[2] * meet]
    up = [high[0] + e_h * down[0], high[1] + e_h * down[1], e_h * down[2], high[2] + e_h * down[3]]
    for i in range(half):
        j, k = half - 1 - i, half + i
        if i > 0:
            e_l, e_h = ratio[j : j + 1, :], ratio[k : k + 1, :]
            down = [
                base[0, j : j + 1, :] + e_l * down[0],
                base[1, j : j + 1, :] + e_l * down[1],
                left[j : j + 1, :] + e_l * down[2],
                e_l * down[3],
            ]
            up = [
                base[0, k : k + 1, :] + e_h * up[0],
                base[1, k : k + 1, :] + e_h * up[1],
                e_h * up[2],
                right[k : k + 1, :] + e_h * up[3],
            ]
        for row, value in ((j, down), (k, up)):
            base[0, row : row + 1, :] = value[0]
            base[1, row : row + 1, :] = value[1]
            left[row : row + 1, :] = value[2]
            right[row : row + 1, :] = value[3]
    inv_top = 1.0 / top
    told = jnp.concatenate(
        [
            down[0],
            down[1],
            up[0] + edge[0:1, :] * inv_top,
            up[1] + edge[1:2, :] * inv_top,
            down[2],
            down[3],
            up[3],
            top,
        ],
        0,
    )
    for step in range(steps):
        send[8 * step : 8 * step + 8, :] = told


def couple(nodes, per, steps, got, base, left, right, send, chain):
    cols = left.shape[1]
    rank = lax.axis_index("gy")

    def told(block, i):
        return got[8 * block + i : 8 * block + i + 1, :]

    zero = jnp.zeros((1, cols), F32)
    g, offset, rho = zero, (zero, zero), zero
    for block in range(steps):
        a, b, c = told(block, 4), told(block, 5), told(block, 6)
        first = [told(block, 0), told(block, 1)]
        last = [told(block, 2), told(block, 3)]
        pushed = [g * offset[0], g * offset[1]]
        kappa = zero if block == 0 else g * (g * rho - 1.0) + STANDIN
        inv = 1.0 / (1.0 - a * kappa)
        start = [(first[i] + a * pushed[i]) * inv for i in range(2)]
        slope = b * inv
        for i, value in enumerate([start[0], start[1], slope, pushed[0], pushed[1], kappa]):
            chain[block, i : i + 1, :] = value
        offset = [last[i] + b * (pushed[i] + kappa * start[i]) for i in range(2)]
        rho = c + b * kappa * slope
        g = told(block, 7)
    value = (zero, zero)
    for block in reversed(range(steps)):
        g = zero if block == steps - 1 else told(block, 7)
        chain[block, 6:7, :] = value[0]
        chain[block, 7:8, :] = value[1]
        value = [chain[block, i : i + 1, :] + chain[block, 2:3, :] * (g * value[i]) for i in range(2)]
    mine = chain[rank]
    own = got[pl.ds(pl.multiple_of(8 * rank, 8), 8), :]
    g_above = jnp.where(rank == steps - 1, 0.0, own[7:8])
    for part in range(2):
        upper = g_above * mine[6 + part : 7 + part]
        here = mine[part : part + 1] + mine[2:3] * upper
        lower = mine[3 + part : 4 + part] + mine[5:6] * here
        for t in range(per):
            rows = pl.ds(t * nodes, nodes)
            solved = base[part, rows, :] + left[rows, :] * lower + right[rows, :] * upper
            send[pl.ds(part * per + t, nodes, stride=SEND_C), :] = solved
        send[pl.ds(2 * per + part, nodes, stride=SEND_C), :] = jnp.broadcast_to(
            mine[6 + part : 7 + part], (nodes, cols)
        )


def inverse(nodes, per, got, across, along, turn, send, edge, pick):
    cols = got.shape[1]
    rank = lax.axis_index("gx")

    def slot(s):
        return got[pl.ds(s, nodes, stride=SEND_C), :]

    kx = wavenumbers(nodes, cols)
    flow, plain = [], []
    for t in range(per):
        real, imag = slot(t), slot(per + t)
        flow.append(jnp.concatenate([-kx * imag, kx * real], 1))
        plain.append(jnp.concatenate([real, imag], 1))
    over = [jnp.concatenate([slot(2 * per), slot(2 * per + 1)], 1)]
    begun = dot(jnp.concatenate(flow + plain + over, 0), along[...])
    c, s = turn[0], turn[1]
    real, imag = [], []
    for i in range(2 * per + 1):
        a = begun[i * nodes : (i + 1) * nodes, :cols]
        b = begun[i * nodes : (i + 1) * nodes, cols:]
        real.append(a * c - b * s)
        imag.append(b * c + a * s)
    both = jnp.concatenate([jnp.concatenate(real, 1), jnp.concatenate(imag, 1)], 0)
    done = dot(across[...], both)
    for i in range(2):
        for part in range(2):
            for t in range(per):
                block = done[part * nodes : (part + 1) * nodes, (i * per + t) * cols : (i * per + t + 1) * cols]
                send[pl.ds((2 * i + part) * per + t, nodes, stride=SEND_D), :] = block
    for extra in range(4 * per, SEND_D):
        send[pl.ds(extra, nodes, stride=SEND_D), :] = jnp.zeros((nodes, cols), F32)
    pick[...] = done[:, 2 * per * cols :]
    for part in range(2):
        edge[part : part + 1, :] = pick[pl.ds(rank + part * nodes, 1), :]


def finish(nodes, per, steps, u, v, w, got, edge, heavy, u_new, v_new, w_new, pot):
    rows, cols = heavy.shape
    rank = lax.axis_index("gy")

    def slot(s):
        return got[pl.ds(s, nodes, stride=SEND_D), :]

    for part in range(2):
        for t in range(per):
            place = pl.ds(t * nodes, nodes)
            u_new[part, place, :] = u[part, place, :] - slot(part * per + t)
            pot[part, place, :] = slot((2 + part) * per + t)
    row = lax.broadcasted_iota(jnp.int32, (rows, cols), 0)
    g = jnp.where((row == rows - 1) & (rank == steps - 1), 0.0, heavy[...])
    for part in range(2):
        here = pot[part]
        after = jnp.where(row == rows - 1, jnp.broadcast_to(edge[part : part + 1, :], (rows, cols)), pltpu.roll(here, rows - 1, 0))
        v_new[part] = v[part] - g * (after - here)
        turned = KZ * pot[1 - part]
        w_new[part] = w[part] + (turned if part == 0 else -turned)


def call(body, outs, scratch, count, flops=1000000):
    return pl.pallas_call(
        body,
        out_shape=[jax.ShapeDtypeStruct(shape, F32) for shape in outs],
        in_specs=[VMEM] * count,
        out_specs=[VMEM] * len(outs),
        scratch_shapes=[pltpu.VMEM(shape, F32) for shape in scratch],
        compiler_params=pltpu.CompilerParams(vmem_limit_bytes=32 * 1024 * 1024),
        cost_estimate=pl.CostEstimate(flops=flops, bytes_accessed=1000000, transcendentals=0),
    )


def exchange(array, axis, count):
    shape = array.shape
    array = array.reshape(count, shape[0] // count, shape[1])
    return lax.all_to_all(array, axis, 0, 0, tiled=True).reshape(shape)


def per_device(u_star, v_star, w_star, cell_width, face_weight):
    nodes, steps = lax.axis_size("gx"), lax.axis_size("gy")
    shape = u_star.shape
    rows, cols = shape[2:]
    per = rows // nodes
    across_f, across_i, along_f, along_i, turn = tables(nodes, cols)
    u, v, w = (x.reshape(2, rows, cols) for x in (u_star, v_star, w_star))
    field, plane = (2, rows, cols), (rows, cols)

    send, wide, heavy = call(
        functools.partial(prepare, nodes), [(nodes * SEND_A, cols), plane, plane], [(4, rows, cols)], 5
    )(u, v, w, cell_width.reshape(1, rows), face_weight.reshape(1, rows))
    got = exchange(send, "gx", nodes)
    send, edge = call(
        functools.partial(forward, nodes, per), [(nodes * SEND_B, cols), (8, cols)], [(nodes, 2 * cols)], 4
    )(got, across_f, along_f, turn)
    got = exchange(send, "gx", nodes)
    base, left, right, send = call(
        functools.partial(eliminate, nodes, per), [field, plane, plane, (8 * steps, cols)], [field, plane], 4
    )(got, edge, wide, heavy)
    got = exchange(send, "gy", steps)
    (send,) = call(
        functools.partial(couple, nodes, per, steps), [(nodes * SEND_C, cols)], [(steps, 8, cols)], 4
    )(got, base, left, right)
    got = exchange(send, "gx", nodes)
    send, edge = call(
        functools.partial(inverse, nodes, per), [(nodes * SEND_D, cols), (8, cols)], [(2 * nodes, cols)], 4
    )(got, across_i, along_i, turn)
    got = exchange(send, "gx", nodes)
    outs = call(functools.partial(finish, nodes, per, steps), [field] * 3, [field], 6)(u, v, w, got, edge, heavy)
    return tuple(x.reshape(shape) for x in outs)


def solution(mesh):
    whole = P(None, None, "gy", "gx")
    return jax.shard_map(
        per_device,
        mesh=mesh,
        in_specs=(whole, whole, whole, P("gy"), P("gy")),
        out_specs=(whole, whole, whole),
        check_vma=False,
    )
```

```python
import functools
import math

import jax
import jax.numpy as jnp
import numpy as np
from jax import lax
from jax.experimental import pallas as pl
from jax.experimental.pallas import tpu as pltpu
from jax.sharding import PartitionSpec as P

FLOW_FACTOR = 0.5
SPAN_FACTOR = 1.0
KZ = SPAN_FACTOR
STANDIN = 16.0
HIGHEST = lax.Precision.HIGHEST
F32 = jnp.float32
VMEM = pl.BlockSpec(memory_space=pltpu.VMEM)
HBM = pl.BlockSpec(memory_space=pltpu.HBM)
SEND_A, SEND_B, SEND_C, SEND_D = 14, 6, 8, 12


def tables(nodes, cols):
    full = nodes * cols

    def cos_sin(a, b, length):
        angle = 2.0 * np.pi * (np.outer(np.arange(a), np.arange(b)) % length) / length
        return np.cos(angle), np.sin(angle)

    c, s = cos_sin(nodes, nodes, nodes)
    across_f = np.block([[c, s], [-s, c]])
    across_i = np.block([[c, -s], [s, c]])
    c, s = cos_sin(cols, cols, cols)
    along_f = np.block([[c, -s], [s, c]])
    along_i = np.block([[c, s], [-s, c]]) / full
    turn = np.stack(cos_sin(nodes, cols, full))
    return [np.asarray(m, np.float32) for m in (across_f, across_i, along_f, along_i, turn)]


def dot(a, b):
    return lax.dot_general(a, b, (((1,), (0,)), ((), ())), precision=HIGHEST, preferred_element_type=F32)


def signed_half(wave, full):
    return jnp.where(wave < full // 2, wave, wave - full).astype(F32) * FLOW_FACTOR


def wavenumbers(nodes, cols):
    rank = lax.broadcasted_iota(jnp.int32, (nodes, cols), 0)
    place = lax.broadcasted_iota(jnp.int32, (nodes, cols), 1)
    return signed_half(rank + nodes * place, nodes * cols)


def column(row, rows, cols):
    here = lax.broadcasted_iota(jnp.int32, (rows, rows), 0)
    there = lax.broadcasted_iota(jnp.int32, (rows, rows), 1)
    one = jnp.sum(jnp.where(here == there, jnp.broadcast_to(row, (rows, rows)), 0.0), axis=1, keepdims=True)
    return jnp.broadcast_to(one, (rows, cols))


def prepare(nodes, u_far, v_far, w_far, width_far, weight_far, send, wide, heavy, u, v, w, width, weight, tmp, arrived):
    rows, cols = u.shape[1:]
    per = rows // nodes
    copies = [
        pltpu.make_async_copy(far, near, arrived.at[i])
        for i, (far, near) in enumerate(
            ((width_far, width), (weight_far, weight), (u_far, u), (w_far, w), (v_far, v))
        )
    ]
    for copy in copies:
        copy.start()
    copies[0].wait()
    h = column(width[...], rows, cols)
    wide[...] = h
    copies[1].wait()
    heavy[...] = column(weight[...], rows, cols)
    copies[2].wait()
    for part in range(2):
        tmp[part] = -h * u[part]
    copies[3].wait()
    copies[4].wait()
    first = lax.broadcasted_iota(jnp.int32, (rows, cols), 0) == 0
    for part in range(2):
        now = v[part]
        below = jnp.where(first, 0.0, pltpu.roll(now, 1, 0))
        other = w[1 - part] * (h * KZ)
        tmp[2 + part] = below - now + (other if part == 0 else -other)
    for field in range(4):
        for t in range(per):
            send[pl.ds(field * per + t, nodes, stride=SEND_A), :] = tmp[field, pl.ds(t * nodes, nodes), :]
    for part in range(2):
        last = jnp.broadcast_to(v[part, rows - 1 : rows, :], (nodes, cols))
        send[pl.ds(4 * per + part, nodes, stride=SEND_A), :] = last


def forward(nodes, per, got, across, along, turn, send, edge, pick):
    cols = got.shape[1]
    rank = lax.axis_index("gx")

    def slot(s):
        return got[pl.ds(s, nodes, stride=SEND_A), :]

    real = [slot(t) for t in range(per)] + [slot(2 * per + t) for t in range(per)] + [slot(4 * per)]
    imag = [slot(per + t) for t in range(per)] + [slot(3 * per + t) for t in range(per)] + [slot(4 * per + 1)]
    both = jnp.concatenate([jnp.concatenate(real, 1), jnp.concatenate(imag, 1)], 0)
    mixed = dot(across[...], both)
    c, s = turn[0], turn[1]
    turned = []
    for i in range(2 * per + 1):
        a = mixed[:nodes, i * cols : (i + 1) * cols]
        b = mixed[nodes:, i * cols : (i + 1) * cols]
        turned.append(jnp.concatenate([a * c + b * s, b * c - a * s], 1))
    pick[...] = turned[-1]
    mine = jnp.broadcast_to(pick[pl.ds(rank, 1), :], (8, 2 * cols))
    spectrum = dot(jnp.concatenate(turned[:-1] + [mine], 0), along[...])
    kx = wavenumbers(nodes, cols)
    for t in range(per):
        u = spectrum[t * nodes : (t + 1) * nodes]
        g = spectrum[(per + t) * nodes : (per + t + 1) * nodes]
        send[pl.ds(t, nodes, stride=SEND_B), :] = g[:, :cols] - kx * u[:, cols:]
        send[pl.ds(per + t, nodes, stride=SEND_B), :] = g[:, cols:] + kx * u[:, :cols]
    for part in range(2):
        edge[part : part + 1, :] = spectrum[2 * per * nodes : 2 * per * nodes + 1, part * cols : (part + 1) * cols]


def eliminate(nodes, per, got, edge, wide, heavy, base, left, right, send, rhs, ratio):
    rows, cols = wide.shape
    steps = lax.axis_size("gy")
    rank_x, rank_y = lax.axis_index("gx"), lax.axis_index("gy")
    for part in range(2):
        for t in range(per):
            rhs[part, pl.ds(t * nodes, nodes), :] = got[pl.ds(part * per + t, nodes, stride=SEND_B), :]
    place = lax.broadcasted_iota(jnp.int32, (1, cols), 1)
    kx = signed_half(rank_x + nodes * place, nodes * cols)
    square = kx * kx + KZ * KZ
    top = heavy[rows - 1 : rows, :]
    above_last = jnp.where(rank_y == steps - 1, 0.0, top)
    below_first = jnp.where(rank_y == 0, 0.0, jnp.full((1, cols), STANDIN, F32))

    def above(j):
        return above_last if j == rows - 1 else heavy[j : j + 1, :]

    def below(j):
        return below_first if j == 0 else heavy[j - 1 : j, :]

    def diagonal(j):
        return above(j) + below(j) + square * wide[j : j + 1, :]

    half = rows // 2
    low = high = None
    for i in range(half):
        j, k = i, rows - 1 - i
        if i == 0:
            inv_l, inv_h = 1.0 / diagonal(j), 1.0 / diagonal(k)
            low = (rhs[0, j : j + 1, :] * inv_l, rhs[1, j : j + 1, :] * inv_l, inv_l)
            high = (rhs[0, k : k + 1, :] * inv_h, rhs[1, k : k + 1, :] * inv_h, inv_h)
        else:
            gl, gh = below(j), above(k)
            inv_l = 1.0 / (diagonal(j) - gl * gl * inv_l)
            inv_h = 1.0 / (diagonal(k) - gh * gh * inv_h)
            low = (
                (rhs[0, j : j + 1, :] + gl * low[0]) * inv_l,
                (rhs[1, j : j + 1, :] + gl * low[1]) * inv_l,
                gl * low[2] * inv_l,
            )
            high = (
                (rhs[0, k : k + 1, :] + gh * high[0]) * inv_h,
                (rhs[1, k : k + 1, :] + gh * high[1]) * inv_h,
                gh * high[2] * inv_h,
            )
        e_l, e_h = above(j) * inv_l, below(k) * inv_h
        if i < half - 1:
            ratio[j : j + 1, :] = e_l
            ratio[k : k + 1, :] = e_h
            for part in range(2):
                base[part, j : j + 1, :] = low[part]
                base[part, k : k + 1, :] = high[part]
            left[j : j + 1, :] = low[2]
            right[k : k + 1, :] = high[2]
    meet = 1.0 / (1.0 - e_l * e_h)
    down = [(low[0] + e_l * high[0]) * meet, (low[1] + e_l * high[1]) * meet, low[2] * meet, e_l * high[2] * meet]
    up = [high[0] + e_h * down[0], high[1] + e_h * down[1], e_h * down[2], high[2] + e_h * down[3]]
    for i in range(half):
        j, k = half - 1 - i, half + i
        if i > 0:
            e_l, e_h = ratio[j : j + 1, :], ratio[k : k + 1, :]
            down = [
                base[0, j : j + 1, :] + e_l * down[0],
                base[1, j : j + 1, :] + e_l * down[1],
                left[j : j + 1, :] + e_l * down[2],
                e_l * down[3],
            ]
            up = [
                base[0, k : k + 1, :] + e_h * up[0],
                base[1, k : k + 1, :] + e_h * up[1],
                e_h * up[2],
                right[k : k + 1, :] + e_h * up[3],
            ]
        for row, value in ((j, down), (k, up)):
            base[0, row : row + 1, :] = value[0]
            base[1, row : row + 1, :] = value[1]
            left[row : row + 1, :] = value[2]
            right[row : row + 1, :] = value[3]
    inv_top = 1.0 / top
    told = jnp.concatenate(
        [
            down[0],
            down[1],
            up[0] + edge[0:1, :] * inv_top,
            up[1] + edge[1:2, :] * inv_top,
            down[2],
            down[3],
            up[3],
            top,
        ],
        0,
    )
    for step in range(steps):
        send[8 * step : 8 * step + 8, :] = told


def couple(nodes, per, steps, got, base, left, right, send, chain):
    cols = left.shape[1]
    rank = lax.axis_index("gy")

    def told(block, i):
        return got[8 * block + i : 8 * block + i + 1, :]

    zero = jnp.zeros((1, cols), F32)
    g, offset, rho = zero, (zero, zero), zero
    for block in range(steps):
        a, b, c = told(block, 4), told(block, 5), told(block, 6)
        first = [told(block, 0), told(block, 1)]
        last = [told(block, 2), told(block, 3)]
        pushed = [g * offset[0], g * offset[1]]
        kappa = zero if block == 0 else g * (g * rho - 1.0) + STANDIN
        inv = 1.0 / (1.0 - a * kappa)
        start = [(first[i] + a * pushed[i]) * inv for i in range(2)]
        slope = b * inv
        for i, value in enumerate([start[0], start[1], slope, pushed[0], pushed[1], kappa]):
            chain[block, i : i + 1, :] = value
        offset = [last[i] + b * (pushed[i] + kappa * start[i]) for i in range(2)]
        rho = c + b * kappa * slope
        g = told(block, 7)
    value = (zero, zero)
    for block in reversed(range(steps)):
        g = zero if block == steps - 1 else told(block, 7)
        chain[block, 6:7, :] = value[0]
        chain[block, 7:8, :] = value[1]
        value = [chain[block, i : i + 1, :] + chain[block, 2:3, :] * (g * value[i]) for i in range(2)]
    mine = chain[rank]
    own = got[pl.ds(pl.multiple_of(8 * rank, 8), 8), :]
    g_above = jnp.where(rank == steps - 1, 0.0, own[7:8])
    for part in range(2):
        upper = g_above * mine[6 + part : 7 + part]
        here = mine[part : part + 1] + mine[2:3] * upper
        lower = mine[3 + part : 4 + part] + mine[5:6] * here
        for t in range(per):
            rows = pl.ds(t * nodes, nodes)
            solved = base[part, rows, :] + left[rows, :] * lower + right[rows, :] * upper
            send[pl.ds(part * per + t, nodes, stride=SEND_C), :] = solved
        send[pl.ds(2 * per + part, nodes, stride=SEND_C), :] = jnp.broadcast_to(
            mine[6 + part : 7 + part], (nodes, cols)
        )


def inverse(nodes, per, got, across, along, turn, send, edge, pick):
    cols = got.shape[1]
    rank = lax.axis_index("gx")

    def slot(s):
        return got[pl.ds(s, nodes, stride=SEND_C), :]

    kx = wavenumbers(nodes, cols)
    flow, plain = [], []
    for t in range(per):
        real, imag = slot(t), slot(per + t)
        flow.append(jnp.concatenate([-kx * imag, kx * real], 1))
        plain.append(jnp.concatenate([real, imag], 1))
    over = [jnp.concatenate([slot(2 * per), slot(2 * per + 1)], 1)]
    begun = dot(jnp.concatenate(flow + plain + over, 0), along[...])
    c, s = turn[0], turn[1]
    real, imag = [], []
    for i in range(2 * per + 1):
        a = begun[i * nodes : (i + 1) * nodes, :cols]
        b = begun[i * nodes : (i + 1) * nodes, cols:]
        real.append(a * c - b * s)
        imag.append(b * c + a * s)
    both = jnp.concatenate([jnp.concatenate(real, 1), jnp.concatenate(imag, 1)], 0)
    done = dot(across[...], both)
    for i in range(2):
        for part in range(2):
            for t in range(per):
                block = done[part * nodes : (part + 1) * nodes, (i * per + t) * cols : (i * per + t + 1) * cols]
                send[pl.ds((2 * i + part) * per + t, nodes, stride=SEND_D), :] = block
    pick[...] = done[:, 2 * per * cols :]
    for part in range(2):
        edge[part : part + 1, :] = pick[pl.ds(rank + part * nodes, 1), :]


def finish(nodes, per, steps, u, v, w, got, edge, heavy, u_far, v_far, w_far, u_new, v_new, w_new, pot, left):
    rows, cols = heavy.shape
    rank = lax.axis_index("gy")
    copies = [
        pltpu.make_async_copy(near.at[part], far.at[part], left.at[2 * i + part])
        for i, (near, far) in enumerate(((u_new, u_far), (w_new, w_far), (v_new, v_far)))
        for part in range(2)
    ]

    def slot(s):
        return got[pl.ds(s, nodes, stride=SEND_D), :]

    for part in range(2):
        for t in range(per):
            place = pl.ds(t * nodes, nodes)
            u_new[part, place, :] = u[part, place, :] - slot(part * per + t)
        copies[part].start()
    for part in range(2):
        for t in range(per):
            pot[part, pl.ds(t * nodes, nodes), :] = slot((2 + part) * per + t)
    for part in range(2):
        turned = KZ * pot[1 - part]
        w_new[part] = w[part] + (turned if part == 0 else -turned)
        copies[2 + part].start()
    row = lax.broadcasted_iota(jnp.int32, (rows, cols), 0)
    g = jnp.where((row == rows - 1) & (rank == steps - 1), 0.0, heavy[...])
    for part in range(2):
        here = pot[part]
        above = jnp.broadcast_to(edge[part : part + 1, :], (rows, cols))
        after = jnp.where(row == rows - 1, above, pltpu.roll(here, rows - 1, 0))
        v_new[part] = v[part] - g * (after - here)
        copies[4 + part].start()
    for copy in copies:
        copy.wait()


def call(body, outs, scratch, ins, out_spec=VMEM, semaphores=0, limit=24):
    scratch = [pltpu.VMEM(shape, F32) for shape in scratch]
    if semaphores:
        scratch.append(pltpu.SemaphoreType.DMA((semaphores,)))
    return pl.pallas_call(
        body,
        out_shape=[jax.ShapeDtypeStruct(shape, F32) for shape in outs],
        in_specs=ins,
        out_specs=[out_spec] * len(outs),
        scratch_shapes=scratch,
        compiler_params=pltpu.CompilerParams(vmem_limit_bytes=limit * 1024 * 1024),
        cost_estimate=pl.CostEstimate(flops=1000000, bytes_accessed=1000000, transcendentals=0),
    )


def exchange(array, axis, count):
    shape = array.shape
    array = array.reshape(count, shape[0] // count * shape[1])
    return lax.all_to_all(array, axis, 0, 0, tiled=True).reshape(shape)


def per_device(u_star, v_star, w_star, cell_width, face_weight):
    nodes, steps = lax.axis_size("gx"), lax.axis_size("gy")
    shape = u_star.shape
    rows, cols = shape[2:]
    per = rows // nodes
    across_f, across_i, along_f, along_i, turn = tables(nodes, cols)
    u, v, w = (x.reshape(2, rows, cols) for x in (u_star, v_star, w_star))
    field, plane, line = (2, rows, cols), (rows, cols), (1, rows)

    send, wide, heavy = call(
        functools.partial(prepare, nodes),
        [(nodes * SEND_A, cols), plane, plane],
        [field, field, field, line, line, (4, rows, cols)],
        [HBM] * 5,
        semaphores=5,
        limit=60,
    )(u, v, w, cell_width.reshape(line), face_weight.reshape(line))
    got = exchange(send, "gx", nodes)
    send, edge = call(
        functools.partial(forward, nodes, per), [(nodes * SEND_B, cols), (8, cols)], [(nodes, 2 * cols)], [VMEM] * 4
    )(got, across_f, along_f, turn)
    got = exchange(send, "gx", nodes)
    base, left, right, send = call(
        functools.partial(eliminate, nodes, per),
        [field, plane, plane, (8 * steps, cols)],
        [field, plane],
        [VMEM] * 4,
    )(got, edge, wide, heavy)
    got = exchange(send, "gy", steps)
    (send,) = call(
        functools.partial(couple, nodes, per, steps), [(nodes * SEND_C, cols)], [(steps, 8, cols)], [VMEM] * 4
    )(got, base, left, right)
    got = exchange(send, "gx", nodes)
    send, edge = call(
        functools.partial(inverse, nodes, per), [(nodes * SEND_D, cols), (8, cols)], [(2 * nodes, cols)], [VMEM] * 4
    )(got, across_i, along_i, turn)
    got = exchange(send, "gx", nodes)
    outs = call(
        functools.partial(finish, nodes, per, steps),
        [field] * 3,
        [field] * 4,
        [VMEM] * 6,
        out_spec=HBM,
        semaphores=6,
    )(u, v, w, got, edge, heavy)
    return tuple(x.reshape(shape) for x in outs)


def solution(mesh):
    whole = P(None, None, "gy", "gx")
    return jax.shard_map(
        per_device,
        mesh=mesh,
        in_specs=(whole, whole, whole, P("gy"), P("gy")),
        out_specs=(whole, whole, whole),
        check_vma=False,
    )
```

```python
import functools
import math

import jax
import jax.numpy as jnp
import numpy as np
from jax import lax
from jax.experimental import pallas as pl
from jax.experimental.pallas import tpu as pltpu
from jax.sharding import PartitionSpec as P

FLOW_FACTOR = 0.5
SPAN_FACTOR = 1.0
KZ = SPAN_FACTOR
STANDIN = 16.0
HIGH, HIGHEST = lax.Precision.HIGH, lax.Precision.HIGHEST
F32 = jnp.float32
VMEM = pl.BlockSpec(memory_space=pltpu.VMEM)
HBM = pl.BlockSpec(memory_space=pltpu.HBM)
ALONG, BESIDE = 4, 4
GROUP = ALONG * BESIDE
SEND_C, SEND_D = 8, 12


def order(nodes):
    breadth = nodes // ALONG
    return [
        breadth * x + BESIDE * q + y for q in range(breadth // BESIDE) for y in range(BESIDE) for x in range(ALONG)
    ]


def place_of(nodes):
    rank = lax.axis_index("gx")
    x, y = rank // (nodes // ALONG), rank % (nodes // ALONG)
    return y // BESIDE * GROUP + y % BESIDE * ALONG + x


def tables(nodes, cols):
    full = nodes * cols

    def cos_sin(a, b, length):
        angle = 2.0 * np.pi * (np.outer(a, b) % length) / length
        return np.cos(angle), np.sin(angle)

    ranks, residues, places = np.array(order(nodes)), np.arange(nodes), np.arange(cols)
    c, s = cos_sin(residues, ranks, nodes)
    across_f = np.stack(
        [
            np.block([[c[:, i : i + GROUP], s[:, i : i + GROUP]], [-s[:, i : i + GROUP], c[:, i : i + GROUP]]])
            for i in range(0, nodes, GROUP)
        ]
    )
    c, s = cos_sin(ranks, residues, nodes)
    across_i = np.block([[c, -s], [s, c]])
    c, s = cos_sin(places, places, cols)
    along_f = np.block([[c, -s], [s, c]])
    along_i = np.block([[c, s], [-s, c]]) / full
    turn = np.stack(cos_sin(residues, places, full))
    return [np.asarray(m, np.float32) for m in (across_f, across_i, along_f, along_i, turn)]


def dot(a, b, precision=HIGHEST):
    return lax.dot_general(a, b, (((1,), (0,)), ((), ())), precision=precision, preferred_element_type=F32)


def signed_half(wave, full):
    return jnp.where(wave < full // 2, wave, wave - full).astype(F32) * FLOW_FACTOR


def wavenumbers(nodes, cols):
    rank = lax.broadcasted_iota(jnp.int32, (nodes, cols), 0)
    place = lax.broadcasted_iota(jnp.int32, (nodes, cols), 1)
    return signed_half(rank + nodes * place, nodes * cols)


def column(row, rows, cols):
    here = lax.broadcasted_iota(jnp.int32, (rows, rows), 0)
    there = lax.broadcasted_iota(jnp.int32, (rows, rows), 1)
    one = jnp.sum(jnp.where(here == there, jnp.broadcast_to(row, (rows, rows)), 0.0), axis=1, keepdims=True)
    return jnp.broadcast_to(one, (rows, cols))


def prepare(u_far, v_far, w_far, width_far, weight_far, send, wide, heavy, u, v, w, width, weight, tmp, arrived):
    rows, cols = u.shape[1:]
    per = rows // GROUP
    copies = [
        pltpu.make_async_copy(far, near, arrived.at[i])
        for i, (far, near) in enumerate(
            ((width_far, width), (weight_far, weight), (u_far, u), (w_far, w), (v_far, v))
        )
    ]
    for copy in copies:
        copy.start()
    copies[0].wait()
    h = column(width[...], rows, cols)
    wide[...] = h
    copies[1].wait()
    heavy[...] = column(weight[...], rows, cols)
    copies[2].wait()
    for part in range(2):
        tmp[part] = -h * u[part]
    copies[3].wait()
    copies[4].wait()
    first = lax.broadcasted_iota(jnp.int32, (rows, cols), 0) == 0
    for part in range(2):
        now = v[part]
        below = jnp.where(first, 0.0, pltpu.roll(now, 1, 0))
        other = w[1 - part] * (h * KZ)
        tmp[2 + part] = below - now + (other if part == 0 else -other)
    to_each = 4 * per + 2
    for field in range(4):
        for t in range(per):
            send[pl.ds(field * per + t, GROUP, stride=to_each), :] = tmp[field, pl.ds(t * GROUP, GROUP), :]
    for part in range(2):
        last = jnp.broadcast_to(v[part, rows - 1 : rows, :], (GROUP, cols))
        send[pl.ds(4 * per + part, GROUP, stride=to_each), :] = last


def forward(nodes, got, across, along, turn, send):
    cols = got.shape[1]
    per = (got.shape[0] // GROUP - 2) // 4
    group = place_of(nodes) // GROUP

    def slot(s):
        return got[pl.ds(s, GROUP, stride=4 * per + 2), :]

    real = [slot(t) for t in range(per)] + [slot(2 * per + t) for t in range(per)] + [slot(4 * per)]
    imag = [slot(per + t) for t in range(per)] + [slot(3 * per + t) for t in range(per)] + [slot(4 * per + 1)]
    both = jnp.concatenate([jnp.concatenate(real, 1), jnp.concatenate(imag, 1)], 0)
    mixed = dot(across[group], both, HIGH)
    c, s = turn[0], turn[1]
    turned = []
    for i in range(2 * per + 1):
        a = mixed[:nodes, i * cols : (i + 1) * cols]
        b = mixed[nodes:, i * cols : (i + 1) * cols]
        turned.append(jnp.concatenate([a * c + b * s, b * c - a * s], 1))
    spectrum = dot(jnp.concatenate(turned, 0), along[...], HIGH)
    kx = wavenumbers(nodes, cols)
    to_each = 2 * per + 2
    for t in range(per):
        u = spectrum[t * nodes : (t + 1) * nodes]
        g = spectrum[(per + t) * nodes : (per + t + 1) * nodes]
        send[pl.ds(t, nodes, stride=to_each), :] = g[:, :cols] - kx * u[:, cols:]
        send[pl.ds(per + t, nodes, stride=to_each), :] = g[:, cols:] + kx * u[:, :cols]
    last = spectrum[2 * per * nodes :]
    for part in range(2):
        send[pl.ds(2 * per + part, nodes, stride=to_each), :] = last[:, part * cols : (part + 1) * cols]


def eliminate(nodes, got, wide, heavy, base, left, right, send, rhs, ratio):
    rows, cols = wide.shape
    steps = lax.axis_size("gy")
    rank_x, rank_y = place_of(nodes), lax.axis_index("gy")
    per = rows // GROUP
    to_each = 2 * per + 2

    def summed(s, count):
        return sum(got[pl.ds(to_each * i + s, count, stride=to_each), :] for i in range(0, nodes, GROUP))

    for part in range(2):
        for t in range(per):
            rhs[part, pl.ds(t * GROUP, GROUP), :] = summed(part * per + t, GROUP)
    edge = [summed(2 * per + part, 1) for part in range(2)]
    place = lax.broadcasted_iota(jnp.int32, (1, cols), 1)
    kx = signed_half(rank_x + nodes * place, nodes * cols)
    square = kx * kx + KZ * KZ
    top = heavy[rows - 1 : rows, :]
    above_last = jnp.where(rank_y == steps - 1, 0.0, top)
    below_first = jnp.where(rank_y == 0, 0.0, jnp.full((1, cols), STANDIN, F32))

    def above(j):
        return above_last if j == rows - 1 else heavy[j : j + 1, :]

    def below(j):
        return below_first if j == 0 else heavy[j - 1 : j, :]

    def diagonal(j):
        return above(j) + below(j) + square * wide[j : j + 1, :]

    half = rows // 2
    low = high = None
    for i in range(half):
        j, k = i, rows - 1 - i
        if i == 0:
            inv_l, inv_h = 1.0 / diagonal(j), 1.0 / diagonal(k)
            low = (rhs[0, j : j + 1, :] * inv_l, rhs[1, j : j + 1, :] * inv_l, inv_l)
            high = (rhs[0, k : k + 1, :] * inv_h, rhs[1, k : k + 1, :] * inv_h, inv_h)
        else:
            gl, gh = below(j), above(k)
            inv_l = 1.0 / (diagonal(j) - gl * gl * inv_l)
            inv_h = 1.0 / (diagonal(k) - gh * gh * inv_h)
            low = (
                (rhs[0, j : j + 1, :] + gl * low[0]) * inv_l,
                (rhs[1, j : j + 1, :] + gl * low[1]) * inv_l,
                gl * low[2] * inv_l,
            )
            high = (
                (rhs[0, k : k + 1, :] + gh * high[0]) * inv_h,
                (rhs[1, k : k + 1, :] + gh * high[1]) * inv_h,
                gh * high[2] * inv_h,
            )
        e_l, e_h = above(j) * inv_l, below(k) * inv_h
        if i < half - 1:
            ratio[j : j + 1, :] = e_l
            ratio[k : k + 1, :] = e_h
            for part in range(2):
                base[part, j : j + 1, :] = low[part]
                base[part, k : k + 1, :] = high[part]
            left[j : j + 1, :] = low[2]
            right[k : k + 1, :] = high[2]
    meet = 1.0 / (1.0 - e_l * e_h)
    down = [(low[0] + e_l * high[0]) * meet, (low[1] + e_l * high[1]) * meet, low[2] * meet, e_l * high[2] * meet]
    up = [high[0] + e_h * down[0], high[1] + e_h * down[1], e_h * down[2], high[2] + e_h * down[3]]
    for i in range(half):
        j, k = half - 1 - i, half + i
        if i > 0:
            e_l, e_h = ratio[j : j + 1, :], ratio[k : k + 1, :]
            down = [
                base[0, j : j + 1, :] + e_l * down[0],
                base[1, j : j + 1, :] + e_l * down[1],
                left[j : j + 1, :] + e_l * down[2],
                e_l * down[3],
            ]
            up = [
                base[0, k : k + 1, :] + e_h * up[0],
                base[1, k : k + 1, :] + e_h * up[1],
                e_h * up[2],
                right[k : k + 1, :] + e_h * up[3],
            ]
        for row, value in ((j, down), (k, up)):
            base[0, row : row + 1, :] = value[0]
            base[1, row : row + 1, :] = value[1]
            left[row : row + 1, :] = value[2]
            right[row : row + 1, :] = value[3]
    inv_top = 1.0 / top
    told = jnp.concatenate(
        [
            down[0],
            down[1],
            up[0] + edge[0] * inv_top,
            up[1] + edge[1] * inv_top,
            down[2],
            down[3],
            up[3],
            top,
        ],
        0,
    )
    for step in range(steps):
        send[8 * step : 8 * step + 8, :] = told


def couple(nodes, per, steps, got, base, left, right, send, chain):
    cols = left.shape[1]
    rank = lax.axis_index("gy")

    def told(block, i):
        return got[8 * block + i : 8 * block + i + 1, :]

    zero = jnp.zeros((1, cols), F32)
    g, offset, rho = zero, (zero, zero), zero
    for block in range(steps):
        a, b, c = told(block, 4), told(block, 5), told(block, 6)
        first = [told(block, 0), told(block, 1)]
        last = [told(block, 2), told(block, 3)]
        pushed = [g * offset[0], g * offset[1]]
        kappa = zero if block == 0 else g * (g * rho - 1.0) + STANDIN
        inv = 1.0 / (1.0 - a * kappa)
        start = [(first[i] + a * pushed[i]) * inv for i in range(2)]
        slope = b * inv
        for i, value in enumerate([start[0], start[1], slope, pushed[0], pushed[1], kappa]):
            chain[block, i : i + 1, :] = value
        offset = [last[i] + b * (pushed[i] + kappa * start[i]) for i in range(2)]
        rho = c + b * kappa * slope
        g = told(block, 7)
    value = (zero, zero)
    for block in reversed(range(steps)):
        g = zero if block == steps - 1 else told(block, 7)
        chain[block, 6:7, :] = value[0]
        chain[block, 7:8, :] = value[1]
        value = [chain[block, i : i + 1, :] + chain[block, 2:3, :] * (g * value[i]) for i in range(2)]
    mine = chain[rank]
    own = got[pl.ds(pl.multiple_of(8 * rank, 8), 8), :]
    g_above = jnp.where(rank == steps - 1, 0.0, own[7:8])
    for part in range(2):
        upper = g_above * mine[6 + part : 7 + part]
        here = mine[part : part + 1] + mine[2:3] * upper
        lower = mine[3 + part : 4 + part] + mine[5:6] * here
        for t in range(per):
            rows = pl.ds(t * nodes, nodes)
            solved = base[part, rows, :] + left[rows, :] * lower + right[rows, :] * upper
            send[pl.ds(part * per + t, nodes, stride=SEND_C), :] = solved
        send[pl.ds(2 * per + part, nodes, stride=SEND_C), :] = jnp.broadcast_to(
            mine[6 + part : 7 + part], (nodes, cols)
        )


def inverse(nodes, per, got, across, along, turn, send, edge, pick):
    cols = got.shape[1]
    place = place_of(nodes)

    def slot(s):
        return got[pl.ds(s, nodes, stride=SEND_C), :]

    def turned(begun):
        c, s = turn[0], turn[1]
        real, imag = [], []
        for i in range(begun.shape[0] // nodes):
            a = begun[i * nodes : (i + 1) * nodes, :cols]
            b = begun[i * nodes : (i + 1) * nodes, cols:]
            real.append(a * c - b * s)
            imag.append(b * c + a * s)
        return jnp.concatenate([jnp.concatenate(real, 1), jnp.concatenate(imag, 1)], 0)

    kx = wavenumbers(nodes, cols)
    flow, plain = [], []
    for t in range(per):
        real, imag = slot(t), slot(per + t)
        flow.append(jnp.concatenate([-kx * imag, kx * real], 1))
        plain.append(jnp.concatenate([real, imag], 1))
    plain.append(jnp.concatenate([slot(2 * per), slot(2 * per + 1)], 1))
    plain = dot(jnp.concatenate(plain, 0), along[...])
    flow = dot(jnp.concatenate(flow, 0), along[...], HIGH)
    plain = dot(across[...], turned(plain))
    flow = dot(across[...], turned(flow), HIGH)
    for i, done in enumerate((flow, plain)):
        for part in range(2):
            for t in range(per):
                block = done[part * nodes : (part + 1) * nodes, t * cols : (t + 1) * cols]
                send[pl.ds((2 * i + part) * per + t, nodes, stride=SEND_D), :] = block
    pick[...] = plain[:, per * cols :]
    for part in range(2):
        edge[part : part + 1, :] = pick[pl.ds(place + part * nodes, 1), :]


def finish(nodes, per, steps, u, v, w, got, edge, heavy, u_far, v_far, w_far, u_new, v_new, w_new, pot, left):
    rows, cols = heavy.shape
    rank = lax.axis_index("gy")
    copies = [
        pltpu.make_async_copy(near.at[part], far.at[part], left.at[2 * i + part])
        for i, (near, far) in enumerate(((u_new, u_far), (w_new, w_far), (v_new, v_far)))
        for part in range(2)
    ]

    def slot(s):
        return got[pl.ds(s, nodes, stride=SEND_D), :]

    for part in range(2):
        for t in range(per):
            place = pl.ds(t * nodes, nodes)
            u_new[part, place, :] = u[part, place, :] - slot(part * per + t)
        copies[part].start()
    for part in range(2):
        for t in range(per):
            pot[part, pl.ds(t * nodes, nodes), :] = slot((2 + part) * per + t)
    for part in range(2):
        turned = KZ * pot[1 - part]
        w_new[part] = w[part] + (turned if part == 0 else -turned)
        copies[2 + part].start()
    row = lax.broadcasted_iota(jnp.int32, (rows, cols), 0)
    g = jnp.where((row == rows - 1) & (rank == steps - 1), 0.0, heavy[...])
    for part in range(2):
        here = pot[part]
        above = jnp.broadcast_to(edge[part : part + 1, :], (rows, cols))
        after = jnp.where(row == rows - 1, above, pltpu.roll(here, rows - 1, 0))
        v_new[part] = v[part] - g * (after - here)
        copies[4 + part].start()
    for copy in copies:
        copy.wait()


def call(body, outs, scratch, ins, out_spec=VMEM, semaphores=0, limit=24):
    scratch = [pltpu.VMEM(shape, F32) for shape in scratch]
    if semaphores:
        scratch.append(pltpu.SemaphoreType.DMA((semaphores,)))
    return pl.pallas_call(
        body,
        out_shape=[jax.ShapeDtypeStruct(shape, F32) for shape in outs],
        in_specs=ins,
        out_specs=[out_spec] * len(outs),
        scratch_shapes=scratch,
        compiler_params=pltpu.CompilerParams(vmem_limit_bytes=limit * 1024 * 1024),
        cost_estimate=pl.CostEstimate(flops=1000000, bytes_accessed=1000000, transcendentals=0),
    )


def exchange(array, axis, count, groups=None):
    shape = array.shape
    array = array.reshape(count, shape[0] // count * shape[1])
    return lax.all_to_all(array, axis, 0, 0, axis_index_groups=groups, tiled=True).reshape(shape)


def per_device(u_star, v_star, w_star, cell_width, face_weight):
    nodes, steps = lax.axis_size("gx"), lax.axis_size("gy")
    shape = u_star.shape
    rows, cols = shape[2:]
    per, wider = rows // nodes, rows // GROUP
    across_f, across_i, along_f, along_i, turn = tables(nodes, cols)
    u, v, w = (x.reshape(2, rows, cols) for x in (u_star, v_star, w_star))
    field, plane, line = (2, rows, cols), (rows, cols), (1, rows)
    ranks = order(nodes)
    near, all_x = [ranks[i : i + GROUP] for i in range(0, nodes, GROUP)], [ranks]

    send, wide, heavy = call(
        prepare,
        [(GROUP * (4 * wider + 2), cols), plane, plane],
        [field, field, field, line, line, (4, rows, cols)],
        [HBM] * 5,
        semaphores=5,
        limit=60,
    )(u, v, w, cell_width.reshape(line), face_weight.reshape(line))
    got = exchange(send, "gx", GROUP, near)
    (send,) = call(functools.partial(forward, nodes), [(nodes * (2 * wider + 2), cols)], [], [VMEM] * 4)(
        got, across_f, along_f, turn
    )
    got = exchange(send, "gx", nodes, all_x)
    base, left, right, send = call(
        functools.partial(eliminate, nodes),
        [field, plane, plane, (8 * steps, cols)],
        [field, plane],
        [VMEM] * 3,
    )(got, wide, heavy)
    got = exchange(send, "gy", steps)
    (send,) = call(
        functools.partial(couple, nodes, per, steps), [(nodes * SEND_C, cols)], [(steps, 8, cols)], [VMEM] * 4
    )(got, base, left, right)
    got = exchange(send, "gx", nodes, all_x)
    send, edge = call(
        functools.partial(inverse, nodes, per), [(nodes * SEND_D, cols), (8, cols)], [(2 * nodes, cols)], [VMEM] * 4
    )(got, across_i, along_i, turn)
    got = exchange(send, "gx", nodes, all_x)
    outs = call(
        functools.partial(finish, nodes, per, steps),
        [field] * 3,
        [field] * 4,
        [VMEM] * 6,
        out_spec=HBM,
        semaphores=6,
    )(u, v, w, got, edge, heavy)
    return tuple(x.reshape(shape) for x in outs)


def solution(mesh):
    whole = P(None, None, "gy", "gx")
    return jax.shard_map(
        per_device,
        mesh=mesh,
        in_specs=(whole, whole, whole, P("gy"), P("gy")),
        out_specs=(whole, whole, whole),
        check_vma=False,
    )
```

```python
import functools
import math

import jax
import jax.numpy as jnp
import numpy as np
from jax import lax
from jax.experimental import pallas as pl
from jax.experimental.pallas import tpu as pltpu
from jax.sharding import PartitionSpec as P

FLOW_FACTOR = 0.5
SPAN_FACTOR = 1.0
KZ = SPAN_FACTOR
STANDIN = 16.0
HIGH, HIGHEST = lax.Precision.HIGH, lax.Precision.HIGHEST
F32 = jnp.float32
VMEM = pl.BlockSpec(memory_space=pltpu.VMEM)
HBM = pl.BlockSpec(memory_space=pltpu.HBM)
ALONG, BESIDE = 4, 4
GROUP = ALONG * BESIDE
SEND_C, SEND_D = 8, 12


def order(nodes):
    breadth = nodes // ALONG
    return [
        breadth * x + BESIDE * q + y for q in range(breadth // BESIDE) for y in range(BESIDE) for x in range(ALONG)
    ]


def place_of(nodes):
    rank = lax.axis_index("gx")
    x, y = rank // (nodes // ALONG), rank % (nodes // ALONG)
    return y // BESIDE * GROUP + y % BESIDE * ALONG + x


def tables(nodes, cols):
    full = nodes * cols

    def cos_sin(a, b, length):
        angle = 2.0 * np.pi * (np.outer(a, b) % length) / length
        return np.cos(angle), np.sin(angle)

    ranks, residues, places = np.array(order(nodes)), np.arange(nodes), np.arange(cols)
    c, s = cos_sin(residues, ranks, nodes)
    across_f = np.stack(
        [
            np.block([[c[:, i : i + GROUP], s[:, i : i + GROUP]], [-s[:, i : i + GROUP], c[:, i : i + GROUP]]])
            for i in range(0, nodes, GROUP)
        ]
    )
    c, s = cos_sin(ranks, residues, nodes)
    across_i = np.block([[c, -s], [s, c]])
    c, s = cos_sin(places, places, cols)
    along_f = np.block([[c, -s], [s, c]])
    along_i = np.block([[c, s], [-s, c]]) / full
    turn = np.stack(cos_sin(residues, places, full))
    return [np.asarray(m, np.float32) for m in (across_f, across_i, along_f, along_i, turn)]


def dot(a, b, precision=HIGHEST):
    return lax.dot_general(a, b, (((1,), (0,)), ((), ())), precision=precision, preferred_element_type=F32)


def signed_half(wave, full):
    return jnp.where(wave < full // 2, wave, wave - full).astype(F32) * FLOW_FACTOR


def wavenumbers(nodes, cols):
    rank = lax.broadcasted_iota(jnp.int32, (nodes, cols), 0)
    place = lax.broadcasted_iota(jnp.int32, (nodes, cols), 1)
    return signed_half(rank + nodes * place, nodes * cols)


def column(row, rows, cols):
    here = lax.broadcasted_iota(jnp.int32, (rows, rows), 0)
    there = lax.broadcasted_iota(jnp.int32, (rows, rows), 1)
    one = jnp.sum(jnp.where(here == there, jnp.broadcast_to(row, (rows, rows)), 0.0), axis=1, keepdims=True)
    return jnp.broadcast_to(one, (rows, cols))


def prepare(u_far, v_far, w_far, width_far, weight_far, send, wide, heavy, u, v, w, width, weight, tmp, arrived):
    rows, cols = u.shape[1:]
    per = rows // GROUP
    copies = [
        pltpu.make_async_copy(far, near, arrived.at[i])
        for i, (far, near) in enumerate(
            ((width_far, width), (weight_far, weight), (u_far, u), (w_far, w), (v_far, v))
        )
    ]
    for copy in copies:
        copy.start()
    copies[0].wait()
    h = column(width[...], rows, cols)
    wide[...] = h
    copies[1].wait()
    heavy[...] = column(weight[...], rows, cols)
    copies[2].wait()
    for part in range(2):
        tmp[part] = -h * u[part]
    copies[3].wait()
    copies[4].wait()
    first = lax.broadcasted_iota(jnp.int32, (rows, cols), 0) == 0
    for part in range(2):
        now = v[part]
        below = jnp.where(first, 0.0, pltpu.roll(now, 1, 0))
        other = w[1 - part] * (h * KZ)
        tmp[2 + part] = below - now + (other if part == 0 else -other)
    to_each = 4 * per + 2
    for field in range(4):
        for t in range(per):
            send[pl.ds(field * per + t, GROUP, stride=to_each), :] = tmp[field, pl.ds(t * GROUP, GROUP), :]
    for part in range(2):
        last = jnp.broadcast_to(v[part, rows - 1 : rows, :], (GROUP, cols))
        send[pl.ds(4 * per + part, GROUP, stride=to_each), :] = last


def forward(nodes, got, across, along, turn, send):
    cols = got.shape[1]
    per = (got.shape[0] // GROUP - 2) // 4
    group = place_of(nodes) // GROUP

    def slot(s):
        return got[pl.ds(s, GROUP, stride=4 * per + 2), :]

    real = [slot(t) for t in range(per)] + [slot(2 * per + t) for t in range(per)] + [slot(4 * per)]
    imag = [slot(per + t) for t in range(per)] + [slot(3 * per + t) for t in range(per)] + [slot(4 * per + 1)]
    both = jnp.concatenate([jnp.concatenate(real, 1), jnp.concatenate(imag, 1)], 0)
    mixed = dot(across[group], both, HIGH)
    c, s = turn[0], turn[1]
    turned = []
    for i in range(2 * per + 1):
        a = mixed[:nodes, i * cols : (i + 1) * cols]
        b = mixed[nodes:, i * cols : (i + 1) * cols]
        turned.append(jnp.concatenate([a * c + b * s, b * c - a * s], 1))
    spectrum = dot(jnp.concatenate(turned, 0), along[...], HIGH)
    kx = wavenumbers(nodes, cols)
    to_each = 2 * per + 2
    for t in range(per):
        u = spectrum[t * nodes : (t + 1) * nodes]
        g = spectrum[(per + t) * nodes : (per + t + 1) * nodes]
        send[pl.ds(t, nodes, stride=to_each), :] = g[:, :cols] - kx * u[:, cols:]
        send[pl.ds(per + t, nodes, stride=to_each), :] = g[:, cols:] + kx * u[:, :cols]
    last = spectrum[2 * per * nodes :]
    for part in range(2):
        send[pl.ds(2 * per + part, nodes, stride=to_each), :] = last[:, part * cols : (part + 1) * cols]


def eliminate(nodes, got, wide, heavy, base, left, right, send, rhs, ratio):
    rows, cols = wide.shape
    steps = lax.axis_size("gy")
    rank_x, rank_y = place_of(nodes), lax.axis_index("gy")
    per = rows // GROUP
    to_each = 2 * per + 2

    def summed(s, count):
        return sum(got[pl.ds(to_each * i + s, count, stride=to_each), :] for i in range(0, nodes, GROUP))

    for part in range(2):
        for t in range(per):
            rhs[part, pl.ds(t * GROUP, GROUP), :] = summed(part * per + t, GROUP)
    edge = [summed(2 * per + part, 1) for part in range(2)]
    place = lax.broadcasted_iota(jnp.int32, (1, cols), 1)
    kx = signed_half(rank_x + nodes * place, nodes * cols)
    square = kx * kx + KZ * KZ
    top = heavy[rows - 1 : rows, :]
    above_last = jnp.where(rank_y == steps - 1, 0.0, top)
    below_first = jnp.where(rank_y == 0, 0.0, jnp.full((1, cols), STANDIN, F32))

    def above(j):
        return above_last if j == rows - 1 else heavy[j : j + 1, :]

    def below(j):
        return below_first if j == 0 else heavy[j - 1 : j, :]

    def diagonal(j):
        return above(j) + below(j) + square * wide[j : j + 1, :]

    half = rows // 2
    low = high = None
    for i in range(half):
        j, k = i, rows - 1 - i
        if i == 0:
            inv_l, inv_h = 1.0 / diagonal(j), 1.0 / diagonal(k)
            low = (rhs[0, j : j + 1, :] * inv_l, rhs[1, j : j + 1, :] * inv_l, inv_l)
            high = (rhs[0, k : k + 1, :] * inv_h, rhs[1, k : k + 1, :] * inv_h, inv_h)
        else:
            gl, gh = below(j), above(k)
            inv_l = 1.0 / (diagonal(j) - gl * gl * inv_l)
            inv_h = 1.0 / (diagonal(k) - gh * gh * inv_h)
            low = (
                (rhs[0, j : j + 1, :] + gl * low[0]) * inv_l,
                (rhs[1, j : j + 1, :] + gl * low[1]) * inv_l,
                gl * low[2] * inv_l,
            )
            high = (
                (rhs[0, k : k + 1, :] + gh * high[0]) * inv_h,
                (rhs[1, k : k + 1, :] + gh * high[1]) * inv_h,
                gh * high[2] * inv_h,
            )
        e_l, e_h = above(j) * inv_l, below(k) * inv_h
        if i < half - 1:
            ratio[j : j + 1, :] = e_l
            ratio[k : k + 1, :] = e_h
            for part in range(2):
                base[part, j : j + 1, :] = low[part]
                base[part, k : k + 1, :] = high[part]
            left[j : j + 1, :] = low[2]
            right[k : k + 1, :] = high[2]
    meet = 1.0 / (1.0 - e_l * e_h)
    down = [(low[0] + e_l * high[0]) * meet, (low[1] + e_l * high[1]) * meet, low[2] * meet, e_l * high[2] * meet]
    up = [high[0] + e_h * down[0], high[1] + e_h * down[1], e_h * down[2], high[2] + e_h * down[3]]
    for i in range(half):
        j, k = half - 1 - i, half + i
        if i > 0:
            e_l, e_h = ratio[j : j + 1, :], ratio[k : k + 1, :]
            down = [
                base[0, j : j + 1, :] + e_l * down[0],
                base[1, j : j + 1, :] + e_l * down[1],
                left[j : j + 1, :] + e_l * down[2],
                e_l * down[3],
            ]
            up = [
                base[0, k : k + 1, :] + e_h * up[0],
                base[1, k : k + 1, :] + e_h * up[1],
                e_h * up[2],
                right[k : k + 1, :] + e_h * up[3],
            ]
        for row, value in ((j, down), (k, up)):
            base[0, row : row + 1, :] = value[0]
            base[1, row : row + 1, :] = value[1]
            left[row : row + 1, :] = value[2]
            right[row : row + 1, :] = value[3]
    inv_top = 1.0 / top
    told = jnp.concatenate(
        [
            down[0],
            down[1],
            up[0] + edge[0] * inv_top,
            up[1] + edge[1] * inv_top,
            down[2],
            down[3],
            up[3],
            top,
        ],
        0,
    )
    for step in range(steps):
        send[8 * step : 8 * step + 8, :] = told


def couple(nodes, per, steps, got, base, left, right, send, chain):
    cols = left.shape[1]
    rank = lax.axis_index("gy")

    def told(block, i):
        return got[8 * block + i : 8 * block + i + 1, :]

    zero = jnp.zeros((1, cols), F32)
    g, offset, rho = zero, (zero, zero), zero
    for block in range(steps):
        a, b, c = told(block, 4), told(block, 5), told(block, 6)
        first = [told(block, 0), told(block, 1)]
        last = [told(block, 2), told(block, 3)]
        pushed = [g * offset[0], g * offset[1]]
        kappa = zero if block == 0 else g * (g * rho - 1.0) + STANDIN
        inv = 1.0 / (1.0 - a * kappa)
        start = [(first[i] + a * pushed[i]) * inv for i in range(2)]
        slope = b * inv
        for i, value in enumerate([start[0], start[1], slope, pushed[0], pushed[1], kappa]):
            chain[block, i : i + 1, :] = value
        offset = [last[i] + b * (pushed[i] + kappa * start[i]) for i in range(2)]
        rho = c + b * kappa * slope
        g = told(block, 7)
    value = (zero, zero)
    for block in reversed(range(steps)):
        g = zero if block == steps - 1 else told(block, 7)
        chain[block, 6:7, :] = value[0]
        chain[block, 7:8, :] = value[1]
        value = [chain[block, i : i + 1, :] + chain[block, 2:3, :] * (g * value[i]) for i in range(2)]
    mine = chain[rank]
    own = got[pl.ds(pl.multiple_of(8 * rank, 8), 8), :]
    g_above = jnp.where(rank == steps - 1, 0.0, own[7:8])
    for part in range(2):
        upper = g_above * mine[6 + part : 7 + part]
        here = mine[part : part + 1] + mine[2:3] * upper
        lower = mine[3 + part : 4 + part] + mine[5:6] * here
        for t in range(per):
            rows = pl.ds(t * nodes, nodes)
            solved = base[part, rows, :] + left[rows, :] * lower + right[rows, :] * upper
            send[pl.ds(part * per + t, nodes, stride=SEND_C), :] = solved
        send[pl.ds(2 * per + part, nodes, stride=SEND_C), :] = jnp.broadcast_to(
            mine[6 + part : 7 + part], (nodes, cols)
        )


def inverse(nodes, per, got, across, along, turn, send, edge, pick):
    cols = got.shape[1]
    place = place_of(nodes)

    def slot(s):
        return got[pl.ds(s, nodes, stride=SEND_C), :]

    def turned(begun):
        c, s = turn[0], turn[1]
        real, imag = [], []
        for i in range(begun.shape[0] // nodes):
            a = begun[i * nodes : (i + 1) * nodes, :cols]
            b = begun[i * nodes : (i + 1) * nodes, cols:]
            real.append(a * c - b * s)
            imag.append(b * c + a * s)
        return jnp.concatenate([jnp.concatenate(real, 1), jnp.concatenate(imag, 1)], 0)

    kx = wavenumbers(nodes, cols)
    flow, plain = [], []
    for t in range(per):
        real, imag = slot(t), slot(per + t)
        flow.append(jnp.concatenate([-kx * imag, kx * real], 1))
        plain.append(jnp.concatenate([real, imag], 1))
    plain.append(jnp.concatenate([slot(2 * per), slot(2 * per + 1)], 1))
    plain = dot(jnp.concatenate(plain, 0), along[...])
    flow = dot(jnp.concatenate(flow, 0), along[...], HIGH)
    plain = dot(across[...], turned(plain))
    flow = dot(across[...], turned(flow), HIGH)
    for i, done in enumerate((flow, plain)):
        for part in range(2):
            for t in range(per):
                block = done[part * nodes : (part + 1) * nodes, t * cols : (t + 1) * cols]
                send[pl.ds((2 * i + part) * per + t, nodes, stride=SEND_D), :] = block
    pick[...] = plain[:, per * cols :]
    for part in range(2):
        edge[part : part + 1, :] = pick[pl.ds(place + part * nodes, 1), :]


def finish(nodes, per, steps, u, v, w, got, edge, heavy, u_far, v_far, w_far, u_new, v_new, w_new, pot, left):
    rows, cols = heavy.shape
    rank = lax.axis_index("gy")
    copies = [
        pltpu.make_async_copy(near.at[part], far.at[part], left.at[2 * i + part])
        for i, (near, far) in enumerate(((u_new, u_far), (w_new, w_far), (v_new, v_far)))
        for part in range(2)
    ]

    def slot(s):
        return got[pl.ds(s, nodes, stride=SEND_D), :]

    for part in range(2):
        for t in range(per):
            place = pl.ds(t * nodes, nodes)
            u_new[part, place, :] = u[part, place, :] - slot(part * per + t)
        copies[part].start()
    for part in range(2):
        for t in range(per):
            pot[part, pl.ds(t * nodes, nodes), :] = slot((2 + part) * per + t)
    for part in range(2):
        turned = KZ * pot[1 - part]
        w_new[part] = w[part] + (turned if part == 0 else -turned)
        copies[2 + part].start()
    row = lax.broadcasted_iota(jnp.int32, (rows, cols), 0)
    g = jnp.where((row == rows - 1) & (rank == steps - 1), 0.0, heavy[...])
    for part in range(2):
        here = pot[part]
        above = jnp.broadcast_to(edge[part : part + 1, :], (rows, cols))
        after = jnp.where(row == rows - 1, above, pltpu.roll(here, rows - 1, 0))
        v_new[part] = v[part] - g * (after - here)
        copies[4 + part].start()
    for copy in copies:
        copy.wait()


def call(body, outs, scratch, ins, out_spec=VMEM, semaphores=0, limit=24):
    scratch = [pltpu.VMEM(shape, F32) for shape in scratch]
    if semaphores:
        scratch.append(pltpu.SemaphoreType.DMA((semaphores,)))
    return pl.pallas_call(
        body,
        out_shape=[jax.ShapeDtypeStruct(shape, F32) for shape in outs],
        in_specs=ins,
        out_specs=[out_spec] * len(outs),
        scratch_shapes=scratch,
        compiler_params=pltpu.CompilerParams(vmem_limit_bytes=limit * 1024 * 1024),
        cost_estimate=pl.CostEstimate(flops=1000000, bytes_accessed=1000000, transcendentals=0),
    )


def exchange(array, axis, count, groups=None):
    shape = array.shape
    array = array.reshape(count, shape[0] // count * shape[1])
    return lax.all_to_all(array, axis, 0, 0, axis_index_groups=groups, tiled=True).reshape(shape)


def per_device(u_star, v_star, w_star, cell_width, face_weight):
    nodes, steps = lax.axis_size("gx"), lax.axis_size("gy")
    shape = u_star.shape
    rows, cols = shape[2:]
    per, wider = rows // nodes, rows // GROUP
    across_f, across_i, along_f, along_i, turn = tables(nodes, cols)
    u, v, w = (x.reshape(2, rows, cols) for x in (u_star, v_star, w_star))
    field, plane, line = (2, rows, cols), (rows, cols), (1, rows)
    ranks = order(nodes)
    near, all_x = [ranks[i : i + GROUP] for i in range(0, nodes, GROUP)], [ranks]

    send, wide, heavy = call(
        prepare,
        [(GROUP * (4 * wider + 2), cols), plane, plane],
        [field, field, field, line, line, (4, rows, cols)],
        [HBM] * 5,
        semaphores=5,
    )(*(pltpu.with_memory_space_constraint(x, pltpu.HBM) for x in (u, v, w, cell_width.reshape(line), face_weight.reshape(line))))
    got = exchange(send, "gx", GROUP, near)
    (send,) = call(functools.partial(forward, nodes), [(nodes * (2 * wider + 2), cols)], [], [VMEM] * 4)(
        got, across_f, along_f, turn
    )
    got = exchange(send, "gx", nodes, all_x)
    base, left, right, send = call(
        functools.partial(eliminate, nodes),
        [field, plane, plane, (8 * steps, cols)],
        [field, plane],
        [VMEM] * 3,
    )(got, wide, heavy)
    got = exchange(send, "gy", steps)
    (send,) = call(
        functools.partial(couple, nodes, per, steps), [(nodes * SEND_C, cols)], [(steps, 8, cols)], [VMEM] * 4
    )(got, base, left, right)
    got = exchange(send, "gx", nodes, all_x)
    send, edge = call(
        functools.partial(inverse, nodes, per), [(nodes * SEND_D, cols), (8, cols)], [(2 * nodes, cols)], [VMEM] * 4
    )(got, across_i, along_i, turn)
    got = exchange(send, "gx", nodes, all_x)
    outs = call(
        functools.partial(finish, nodes, per, steps),
        [field] * 3,
        [field] * 4,
        [VMEM] * 6,
        out_spec=HBM,
        semaphores=6,
    )(u, v, w, got, edge, heavy)
    return tuple(x.reshape(shape) for x in outs)


def solution(mesh):
    whole = P(None, None, "gy", "gx")
    return jax.shard_map(
        per_device,
        mesh=mesh,
        in_specs=(whole, whole, whole, P("gy"), P("gy")),
        out_specs=(whole, whole, whole),
        check_vma=False,
    )
```

```python
import functools
import math

import jax
import jax.numpy as jnp
import numpy as np
from jax import lax
from jax.experimental import pallas as pl
from jax.experimental.pallas import tpu as pltpu
from jax.sharding import PartitionSpec as P

FLOW_FACTOR = 0.5
SPAN_FACTOR = 1.0
KZ = SPAN_FACTOR
STANDIN = 16.0
F32 = jnp.float32
VMEM = pl.BlockSpec(memory_space=pltpu.VMEM)
HBM = pl.BlockSpec(memory_space=pltpu.HBM)
ALONG, BESIDE = 4, 4
GROUP = ALONG * BESIDE
LEVELS = 3
SEGMENTS = 2**LEVELS
SEND_C, SEND_D = 8, 12


def order(nodes):
    breadth = nodes // ALONG
    return [
        breadth * x + BESIDE * q + y for q in range(breadth // BESIDE) for y in range(BESIDE) for x in range(ALONG)
    ]


def place_of(nodes):
    rank = lax.axis_index("gx")
    x, y = rank // (nodes // ALONG), rank % (nodes // ALONG)
    return y // BESIDE * GROUP + y % BESIDE * ALONG + x


def tables(nodes, cols):
    full = nodes * cols

    def cos_sin(a, b, length):
        angle = 2.0 * np.pi * (np.outer(a, b) % length) / length
        return np.cos(angle), np.sin(angle)

    ranks, residues, places = np.array(order(nodes)), np.arange(nodes), np.arange(cols)
    c, s = cos_sin(residues, ranks, nodes)
    across_f = np.stack(
        [
            np.block([[c[:, i : i + GROUP], s[:, i : i + GROUP]], [-s[:, i : i + GROUP], c[:, i : i + GROUP]]])
            for i in range(0, nodes, GROUP)
        ]
    )
    c, s = cos_sin(ranks, residues, nodes)
    across_i = np.block([[c, -s], [s, c]])
    c, s = cos_sin(places, places, cols)
    along_f = np.block([[c, -s], [s, c]])
    along_i = np.block([[c, s], [-s, c]]) / full
    turn = np.stack(cos_sin(residues, places, full))
    return [
        constant_side(across_f, -1, 2),
        constant_side(across_i, -1, 2),
        constant_side(across_i, -1, 3),
        constant_side(along_f, 0, 2),
        constant_side(along_i, 0, 2),
        constant_side(along_i, 0, 3),
        np.asarray(turn, np.float32),
    ]


def pairs(terms):
    return [(i, j) for i in range(terms) for j in range(terms) if i + j < terms]


def expand(value, terms, one, whole):
    parts = []
    for _ in range(terms):
        parts.append(value.astype(one))
        value = value - parts[-1].astype(whole)
    return parts


def constant_side(matrix, axis, terms):
    parts = expand(np.asarray(matrix, np.float64), terms, jnp.bfloat16, np.float64)
    return np.concatenate([parts[i] for i, _ in pairs(terms)], axis)


def data_side(value, axis, terms):
    parts = expand(value, terms, jnp.bfloat16, F32)
    return jnp.concatenate([parts[j] for _, j in pairs(terms)], axis)


def dot(a, b):
    return lax.dot_general(a, b, (((1,), (0,)), ((), ())), preferred_element_type=F32)


def left_dot(constant, value, terms):
    return dot(constant, data_side(value, 0, terms))


def right_dot(value, constant, terms):
    return dot(data_side(value, 1, terms), constant)


def signed_half(wave, full):
    return jnp.where(wave < full // 2, wave, wave - full).astype(F32) * FLOW_FACTOR


def wavenumbers(nodes, cols):
    rank = lax.broadcasted_iota(jnp.int32, (nodes, cols), 0)
    place = lax.broadcasted_iota(jnp.int32, (nodes, cols), 1)
    return signed_half(rank + nodes * place, nodes * cols)


def column(row, rows, cols):
    here = lax.broadcasted_iota(jnp.int32, (rows, rows), 0)
    there = lax.broadcasted_iota(jnp.int32, (rows, rows), 1)
    one = jnp.sum(jnp.where(here == there, jnp.broadcast_to(row, (rows, rows)), 0.0), axis=1, keepdims=True)
    return jnp.broadcast_to(one, (rows, cols))


def prepare(u_far, v_far, w_far, width_far, weight_far, send, wide, heavy, u, v, w, width, weight, tmp, arrived):
    rows, cols = u.shape[1:]
    per = rows // GROUP
    copies = [
        pltpu.make_async_copy(far, near, arrived.at[i])
        for i, (far, near) in enumerate(
            ((width_far, width), (weight_far, weight), (u_far, u), (w_far, w), (v_far, v))
        )
    ]
    for copy in copies:
        copy.start()
    copies[0].wait()
    h = column(width[...], rows, cols)
    wide[...] = h
    copies[1].wait()
    heavy[...] = column(weight[...], rows, cols)
    copies[2].wait()
    for part in range(2):
        tmp[part] = -h * u[part]
    copies[3].wait()
    copies[4].wait()
    first = lax.broadcasted_iota(jnp.int32, (rows, cols), 0) == 0
    for part in range(2):
        now = v[part]
        below = jnp.where(first, 0.0, pltpu.roll(now, 1, 0))
        other = w[1 - part] * (h * KZ)
        tmp[2 + part] = below - now + (other if part == 0 else -other)
    to_each = 4 * per + 2
    for field in range(4):
        for t in range(per):
            send[pl.ds(field * per + t, GROUP, stride=to_each), :] = tmp[field, pl.ds(t * GROUP, GROUP), :]
    for part in range(2):
        last = jnp.broadcast_to(v[part, rows - 1 : rows, :], (GROUP, cols))
        send[pl.ds(4 * per + part, GROUP, stride=to_each), :] = last


def forward(nodes, got, across, along, turn, send):
    cols = got.shape[1]
    per = (got.shape[0] // GROUP - 2) // 4
    group = place_of(nodes) // GROUP

    def slot(s):
        return got[pl.ds(s, GROUP, stride=4 * per + 2), :]

    real = [slot(t) for t in range(per)] + [slot(2 * per + t) for t in range(per)] + [slot(4 * per)]
    imag = [slot(per + t) for t in range(per)] + [slot(3 * per + t) for t in range(per)] + [slot(4 * per + 1)]
    both = jnp.concatenate([jnp.concatenate(real, 1), jnp.concatenate(imag, 1)], 0)
    mixed = left_dot(across[group], both, 2)
    c, s = turn[0], turn[1]
    turned = []
    for i in range(2 * per + 1):
        a = mixed[:nodes, i * cols : (i + 1) * cols]
        b = mixed[nodes:, i * cols : (i + 1) * cols]
        turned.append(jnp.concatenate([a * c + b * s, b * c - a * s], 1))
    spectrum = right_dot(jnp.concatenate(turned, 0), along[...], 2)
    kx = wavenumbers(nodes, cols)
    to_each = 2 * per + 2
    for t in range(per):
        u = spectrum[t * nodes : (t + 1) * nodes]
        g = spectrum[(per + t) * nodes : (per + t + 1) * nodes]
        send[pl.ds(t, nodes, stride=to_each), :] = g[:, :cols] - kx * u[:, cols:]
        send[pl.ds(per + t, nodes, stride=to_each), :] = g[:, cols:] + kx * u[:, :cols]
    last = spectrum[2 * per * nodes :]
    for part in range(2):
        send[pl.ds(2 * per + part, nodes, stride=to_each), :] = last[:, part * cols : (part + 1) * cols]


def joined(first, last, a, b, c, gap):
    count, joins, span = a.shape[0], [], 1
    while span < count:

        def ahead(value, by):
            return pltpu.roll(value, count - by, 0) if by else value

        g = ahead(gap, span - 1)
        next_first, next_last = [ahead(x, span) for x in first], [ahead(x, span) for x in last]
        next_a, next_b, next_c = ahead(a, span), ahead(b, span), ahead(c, span)
        weight = g / (1.0 - g * g * c * next_a)
        by_l, by_r = b * weight, next_b * weight
        from_below = [(last[n] + c * g * next_first[n]) * weight for n in range(2)]
        from_above = [(next_first[n] + next_a * g * last[n]) * weight for n in range(2)]
        below_r, above_l = c * g * by_r, next_a * g * by_l
        joins.append(from_below + from_above + [by_l, below_r, above_l, by_r])
        first = [first[n] + b * from_above[n] for n in range(2)]
        last = [next_last[n] + next_b * from_below[n] for n in range(2)]
        a, b, c = a + b * above_l, b * by_r, next_c + next_b * below_r
        span *= 2
    return (first, last, a, b, c), joins


def parted(joins, part, lower, upper):
    run = lax.broadcasted_iota(jnp.int32, lower.shape, 0)
    for level in reversed(range(len(joins))):
        join, span = joins[level], 2**level
        later = run // span % 2 == 1
        from_below = join[part] + join[4] * lower + join[5] * upper
        from_above = join[2 + part] + join[6] * lower + join[7] * upper
        lower = jnp.where(later, pltpu.roll(from_below, span, 0), lower)
        upper = jnp.where(later, pltpu.roll(upper, span, 0), from_above)
    return lower, upper


def eliminate(nodes, got, wide, heavy, base, left, right, tree, send, rhs):
    rows, cols = wide.shape
    length = rows // SEGMENTS
    steps = lax.axis_size("gy")
    rank_x, rank_y = place_of(nodes), lax.axis_index("gy")
    per = rows // GROUP
    to_each = 2 * per + 2

    def summed(s, count):
        return sum(got[pl.ds(to_each * i + s, count, stride=to_each), :] for i in range(0, nodes, GROUP))

    for part in range(2):
        for t in range(per):
            rhs[part, pl.ds(t * GROUP, GROUP), :] = summed(part * per + t, GROUP)
    edge = [summed(2 * per + part, 1) for part in range(2)]
    place = lax.broadcasted_iota(jnp.int32, (SEGMENTS, cols), 1)
    run = lax.broadcasted_iota(jnp.int32, (SEGMENTS, cols), 0)
    kx = signed_half(rank_x + nodes * place, nodes * cols)
    square = kx * kx + KZ * KZ
    top = heavy[rows - 1 : rows, :]
    every = [pl.ds(t, SEGMENTS, stride=length) for t in range(length)]
    above = [heavy[rows_t, :] for rows_t in every]
    below = [jnp.where(run == 0, jnp.where(rank_y == 0, 0.0, STANDIN), pltpu.roll(above[-1], 1, 0))] + above[:-1]
    above[-1] = jnp.where((run == SEGMENTS - 1) & (rank_y == steps - 1), 0.0, above[-1])
    diagonal = [above[t] + below[t] + square * wide[every[t], :] for t in range(length)]
    right_side = [[rhs[part, rows_t, :] for part in range(2)] for rows_t in every]

    half = length // 2
    low, high, ratio_l, ratio_h = [], [], [], []
    for i in range(half):
        j, k = i, length - 1 - i
        if i == 0:
            inv_l, inv_h = 1.0 / diagonal[j], 1.0 / diagonal[k]
            low.append([right_side[j][0] * inv_l, right_side[j][1] * inv_l, inv_l])
            high.append([right_side[k][0] * inv_h, right_side[k][1] * inv_h, inv_h])
        else:
            gl, gh = below[j], above[k]
            inv_l = 1.0 / (diagonal[j] - gl * gl * inv_l)
            inv_h = 1.0 / (diagonal[k] - gh * gh * inv_h)
            was_l, was_h = low[-1], high[-1]
            low.append([(right_side[j][n] + gl * was_l[n]) * inv_l for n in range(2)] + [gl * was_l[2] * inv_l])
            high.append([(right_side[k][n] + gh * was_h[n]) * inv_h for n in range(2)] + [gh * was_h[2] * inv_h])
        ratio_l.append(above[j] * inv_l)
        ratio_h.append(below[k] * inv_h)
    e_l, e_h = ratio_l[-1], ratio_h[-1]
    meet = 1.0 / (1.0 - e_l * e_h)
    down = [(low[-1][n] + e_l * high[-1][n]) * meet for n in range(2)] + [low[-1][2] * meet, e_l * high[-1][2] * meet]
    up = [high[-1][n] + e_h * down[n] for n in range(2)] + [e_h * down[2], high[-1][2] + e_h * down[3]]
    for i in reversed(range(half)):
        j, k = i, length - 1 - i
        if i < half - 1:
            e_l, e_h = ratio_l[i], ratio_h[i]
            down = [low[i][n] + e_l * down[n] for n in range(3)] + [e_l * down[3]]
            up = [high[i][n] + e_h * up[n] for n in range(2)] + [e_h * up[2], high[i][2] + e_h * up[3]]
        for t, value in ((j, down), (k, up)):
            here = pl.ds(t * SEGMENTS, SEGMENTS)
            base[0, here, :], base[1, here, :], left[here, :], right[here, :] = value

    (first, last, a, b, c), joins = joined(down[:2], up[:2], down[2], down[3], up[3], above[-1])
    for level, join in enumerate(joins):
        for i, value in enumerate(join):
            tree[level, i] = value
    inv_top = 1.0 / top
    told = [x[:1] for x in first + last + [a, b, c]] + [top]
    for part in range(2):
        told[2 + part] = told[2 + part] + edge[part] * inv_top
    told = jnp.concatenate(told, 0)
    for step in range(steps):
        send[8 * step : 8 * step + 8, :] = told


def couple(nodes, per, steps, got, base, left, right, tree, send, chain):
    cols = left.shape[1]
    rank = lax.axis_index("gy")
    first, last, a, b, c, gap = (
        [got[pl.ds(i, steps, stride=8), :] for i in some] for some in ((0, 1), (2, 3), (4,), (5,), (6,), (7,))
    )
    a, b, c, gap = a[0], b[0], c[0], gap[0]
    block = lax.broadcasted_iota(jnp.int32, (steps, cols), 0)
    change = jnp.where(block == 0, 0.0, pltpu.roll(gap, 1, 0) - STANDIN)
    scale = 1.0 / (1.0 + a * change)
    first = [x * scale for x in first]
    last = [last[n] - b * change * first[n] for n in range(2)]
    a, b, c = a * scale, b * scale, c - b * b * change * scale
    joins = joined(first, last, a, b, c, gap)[1]
    for part in range(2):
        lower, upper = parted(joins, part, jnp.zeros_like(a), jnp.zeros_like(a))
        here = first[part] + a * lower + b * upper
        chain[3 * part] = lower - change * here
        chain[3 * part + 1] = upper
        chain[3 * part + 2] = pltpu.roll(here, steps - 1, 0)
    inner = [[tree[level, i] for i in range(8)] for level in range(LEVELS)]
    length = left.shape[0] // SEGMENTS
    for part in range(2):
        lower, upper, after = (chain[3 * part + i, pl.ds(rank, 1), :] for i in range(3))
        lower, upper = parted(inner, part, *(jnp.broadcast_to(x, (SEGMENTS, cols)) for x in (lower, upper)))
        for t in range(length):
            rows = pl.ds(t * SEGMENTS, SEGMENTS)
            solved = base[part, rows, :] + left[rows, :] * lower + right[rows, :] * upper
            spot = t // per * SEND_C + part * per + t % per
            send[pl.ds(spot, SEGMENTS, stride=length // per * SEND_C), :] = solved
        send[pl.ds(2 * per + part, nodes, stride=SEND_C), :] = jnp.broadcast_to(after, (nodes, cols))


def inverse(nodes, per, got, across, across_full, along, along_full, turn, send, edge, pick):
    cols = got.shape[1]
    place = place_of(nodes)

    def slot(s):
        return got[pl.ds(s, nodes, stride=SEND_C), :]

    def turned(begun):
        c, s = turn[0], turn[1]
        real, imag = [], []
        for i in range(begun.shape[0] // nodes):
            a = begun[i * nodes : (i + 1) * nodes, :cols]
            b = begun[i * nodes : (i + 1) * nodes, cols:]
            real.append(a * c - b * s)
            imag.append(b * c + a * s)
        return jnp.concatenate([jnp.concatenate(real, 1), jnp.concatenate(imag, 1)], 0)

    kx = wavenumbers(nodes, cols)
    flow, plain = [], []
    for t in range(per):
        real, imag = slot(t), slot(per + t)
        flow.append(jnp.concatenate([-kx * imag, kx * real], 1))
        plain.append(jnp.concatenate([real, imag], 1))
    plain.append(jnp.concatenate([slot(2 * per), slot(2 * per + 1)], 1))
    plain = right_dot(jnp.concatenate(plain, 0), along_full[...], 3)
    flow = right_dot(jnp.concatenate(flow, 0), along[...], 2)
    plain = left_dot(across_full[...], turned(plain), 3)
    flow = left_dot(across[...], turned(flow), 2)
    for i, done in enumerate((flow, plain)):
        for part in range(2):
            for t in range(per):
                block = done[part * nodes : (part + 1) * nodes, t * cols : (t + 1) * cols]
                send[pl.ds((2 * i + part) * per + t, nodes, stride=SEND_D), :] = block
    pick[...] = plain[:, per * cols :]
    for part in range(2):
        edge[part : part + 1, :] = pick[pl.ds(place + part * nodes, 1), :]


def finish(nodes, per, steps, u, v, w, got, edge, heavy, u_far, v_far, w_far, u_new, v_new, w_new, pot, left):
    rows, cols = heavy.shape
    rank = lax.axis_index("gy")
    copies = [
        pltpu.make_async_copy(near.at[part], far.at[part], left.at[2 * i + part])
        for i, (near, far) in enumerate(((u_new, u_far), (w_new, w_far), (v_new, v_far)))
        for part in range(2)
    ]

    def slot(s):
        return got[pl.ds(s, nodes, stride=SEND_D), :]

    for part in range(2):
        for t in range(per):
            place = pl.ds(t, nodes, stride=per)
            u_new[part, place, :] = u[part, place, :] - slot(part * per + t)
        copies[part].start()
    for part in range(2):
        for t in range(per):
            pot[part, pl.ds(t, nodes, stride=per), :] = slot((2 + part) * per + t)
    for part in range(2):
        turned = KZ * pot[1 - part]
        w_new[part] = w[part] + (turned if part == 0 else -turned)
        copies[2 + part].start()
    row = lax.broadcasted_iota(jnp.int32, (rows, cols), 0)
    g = jnp.where((row == rows - 1) & (rank == steps - 1), 0.0, heavy[...])
    for part in range(2):
        here = pot[part]
        above = jnp.broadcast_to(edge[part : part + 1, :], (rows, cols))
        after = jnp.where(row == rows - 1, above, pltpu.roll(here, rows - 1, 0))
        v_new[part] = v[part] - g * (after - here)
        copies[4 + part].start()
    for copy in copies:
        copy.wait()


def call(body, outs, scratch, ins, out_spec=VMEM, semaphores=0, limit=24):
    scratch = [pltpu.VMEM(shape, F32) for shape in scratch]
    if semaphores:
        scratch.append(pltpu.SemaphoreType.DMA((semaphores,)))
    return pl.pallas_call(
        body,
        out_shape=[jax.ShapeDtypeStruct(shape, F32) for shape in outs],
        in_specs=ins,
        out_specs=[out_spec] * len(outs),
        scratch_shapes=scratch,
        compiler_params=pltpu.CompilerParams(vmem_limit_bytes=limit * 1024 * 1024),
        cost_estimate=pl.CostEstimate(flops=1000000, bytes_accessed=1000000, transcendentals=0),
    )


def exchange(array, axis, count, groups=None):
    shape = array.shape
    array = array.reshape(count, shape[0] // count * shape[1])
    return lax.all_to_all(array, axis, 0, 0, axis_index_groups=groups, tiled=True).reshape(shape)


def per_device(u_star, v_star, w_star, cell_width, face_weight):
    nodes, steps = lax.axis_size("gx"), lax.axis_size("gy")
    shape = u_star.shape
    rows, cols = shape[2:]
    per, wider = rows // nodes, rows // GROUP
    across_f, across_i, across_full, along_f, along_i, along_full, turn = tables(nodes, cols)
    u, v, w = (x.reshape(2, rows, cols) for x in (u_star, v_star, w_star))
    field, plane, line = (2, rows, cols), (rows, cols), (1, rows)
    ranks = order(nodes)
    near, all_x = [ranks[i : i + GROUP] for i in range(0, nodes, GROUP)], [ranks]

    send, wide, heavy = call(
        prepare,
        [(GROUP * (4 * wider + 2), cols), plane, plane],
        [field, field, field, line, line, (4, rows, cols)],
        [HBM] * 5,
        semaphores=5,
    )(*(pltpu.with_memory_space_constraint(x, pltpu.HBM) for x in (u, v, w, cell_width.reshape(line), face_weight.reshape(line))))
    got = exchange(send, "gx", GROUP, near)
    (send,) = call(functools.partial(forward, nodes), [(nodes * (2 * wider + 2), cols)], [], [VMEM] * 4)(
        got, across_f, along_f, turn
    )
    got = exchange(send, "gx", nodes, all_x)
    base, left, right, tree, send = call(
        functools.partial(eliminate, nodes),
        [field, plane, plane, (LEVELS, 8, SEGMENTS, cols), (8 * steps, cols)],
        [field],
        [VMEM] * 3,
    )(got, wide, heavy)
    got = exchange(send, "gy", steps)
    (send,) = call(
        functools.partial(couple, nodes, per, steps), [(nodes * SEND_C, cols)], [(6, steps, cols)], [VMEM] * 5
    )(got, base, left, right, tree)
    got = exchange(send, "gx", nodes, all_x)
    send, edge = call(
        functools.partial(inverse, nodes, per), [(nodes * SEND_D, cols), (8, cols)], [(2 * nodes, cols)], [VMEM] * 6
    )(got, across_i, across_full, along_i, along_full, turn)
    got = exchange(send, "gx", nodes, all_x)
    outs = call(
        functools.partial(finish, nodes, per, steps),
        [field] * 3,
        [field] * 4,
        [VMEM] * 6,
        out_spec=HBM,
        semaphores=6,
    )(u, v, w, got, edge, heavy)
    return tuple(x.reshape(shape) for x in outs)


def solution(mesh):
    whole = P(None, None, "gy", "gx")
    return jax.shard_map(
        per_device,
        mesh=mesh,
        in_specs=(whole, whole, whole, P("gy"), P("gy")),
        out_specs=(whole, whole, whole),
        check_vma=False,
    )
```

```python
import functools
import math

import jax
import jax.numpy as jnp
import numpy as np
from jax import lax
from jax.experimental import pallas as pl
from jax.experimental.pallas import tpu as pltpu
from jax.sharding import PartitionSpec as P

FLOW_FACTOR = 0.5
SPAN_FACTOR = 1.0
KZ = SPAN_FACTOR
STANDIN = 16.0
F32 = jnp.float32
VMEM = pl.BlockSpec(memory_space=pltpu.VMEM)
HBM = pl.BlockSpec(memory_space=pltpu.HBM)
ALONG, BESIDE = 4, 4
GROUP = ALONG * BESIDE
LEVELS = 3
SEGMENTS = 2**LEVELS


PLACES = [(2, 2), (1, 1), (3, 0), (2, 1), (3, 2), (0, 3), (0, 0), (2, 0), (3, 1), (0, 2), (3, 3), (1, 2), (2, 3), (0, 1), (1, 0), (1, 3)]


def order(nodes):
    breadth = nodes // ALONG
    return [breadth * x + BESIDE * q + y for q in range(breadth // BESIDE) for x, y in PLACES]


def place_of(nodes):
    rank = lax.axis_index("gx")
    return sum(jnp.where(rank == other, place, 0) for place, other in enumerate(order(nodes)))


def tables(nodes, cols):
    full = nodes * cols

    def cos_sin(a, b, length):
        angle = 2.0 * np.pi * (np.outer(a, b) % length) / length
        return np.cos(angle), np.sin(angle)

    ranks, residues, places = np.array(order(nodes)), np.arange(nodes), np.arange(cols)
    c, s = cos_sin(residues, ranks, nodes)
    across_f = np.stack(
        [
            np.block([[c[:, i : i + GROUP], s[:, i : i + GROUP]], [-s[:, i : i + GROUP], c[:, i : i + GROUP]]])
            for i in range(0, nodes, GROUP)
        ]
    )
    c, s = cos_sin(ranks, residues, nodes)
    across_i = np.stack(
        [
            np.block([[c[i : i + GROUP], -s[i : i + GROUP]], [s[i : i + GROUP], c[i : i + GROUP]]])
            for i in range(0, nodes, GROUP)
        ]
    )
    c, s = cos_sin(places, places, cols)
    along_f = np.block([[c, -s], [s, c]])
    along_i = np.block([[c, s], [-s, c]]) / full
    turn = np.stack(cos_sin(residues, places, full))
    return [
        constant_side(across_f, -1, 2),
        constant_side(across_i, -1, 2),
        constant_side(across_i, -1, 3),
        constant_side(along_f, 0, 2),
        constant_side(along_i, 0, 2),
        constant_side(along_i, 0, 3),
        np.asarray(turn, np.float32),
    ]


def pairs(terms):
    return [(i, j) for i in range(terms) for j in range(terms) if i + j < terms]


def expand(value, terms, one, whole):
    parts = []
    for _ in range(terms):
        parts.append(value.astype(one))
        value = value - parts[-1].astype(whole)
    return parts


def constant_side(matrix, axis, terms):
    parts = expand(np.asarray(matrix, np.float64), terms, jnp.bfloat16, np.float64)
    return np.concatenate([parts[i] for i, _ in pairs(terms)], axis)


def data_side(value, axis, terms):
    parts = expand(value, terms, jnp.bfloat16, F32)
    return jnp.concatenate([parts[j] for _, j in pairs(terms)], axis)


def dot(a, b):
    return lax.dot_general(a, b, (((1,), (0,)), ((), ())), preferred_element_type=F32)


def left_dot(constant, value, terms):
    return dot(constant, data_side(value, 0, terms))


def right_dot(value, constant, terms):
    return dot(data_side(value, 1, terms), constant)


def signed_half(wave, full):
    return jnp.where(wave < full // 2, wave, wave - full).astype(F32) * FLOW_FACTOR


def wavenumbers(nodes, cols):
    rank = lax.broadcasted_iota(jnp.int32, (nodes, cols), 0)
    place = lax.broadcasted_iota(jnp.int32, (nodes, cols), 1)
    return signed_half(rank + nodes * place, nodes * cols)


def column(row, rows, cols):
    here = lax.broadcasted_iota(jnp.int32, (rows, rows), 0)
    there = lax.broadcasted_iota(jnp.int32, (rows, rows), 1)
    one = jnp.sum(jnp.where(here == there, jnp.broadcast_to(row, (rows, rows)), 0.0), axis=1, keepdims=True)
    return jnp.broadcast_to(one, (rows, cols))


def prepare(u_far, v_far, w_far, width_far, weight_far, send, wide, heavy, u, v, w, width, weight, tmp, arrived):
    rows, cols = u.shape[1:]
    per = rows // GROUP
    copies = [
        pltpu.make_async_copy(far, near, arrived.at[i])
        for i, (far, near) in enumerate(
            ((width_far, width), (weight_far, weight), (u_far, u), (w_far, w), (v_far, v))
        )
    ]
    for copy in copies:
        copy.start()
    copies[0].wait()
    h = column(width[...], rows, cols)
    wide[...] = h
    copies[1].wait()
    heavy[...] = column(weight[...], rows, cols)
    to_each = 4 * per + 2

    def pack(field):
        for t in range(per):
            send[pl.ds(field * per + t, GROUP, stride=to_each), :] = tmp[field, pl.ds(t * GROUP, GROUP), :]

    copies[2].wait()
    for part in range(2):
        tmp[part] = -h * u[part]
        pack(part)
    copies[3].wait()
    copies[4].wait()
    first = lax.broadcasted_iota(jnp.int32, (rows, cols), 0) == 0
    for part in range(2):
        now = v[part]
        below = jnp.where(first, 0.0, pltpu.roll(now, 1, 0))
        other = w[1 - part] * (h * KZ)
        tmp[2 + part] = below - now + (other if part == 0 else -other)
        pack(2 + part)
        last = jnp.broadcast_to(v[part, rows - 1 : rows, :], (GROUP, cols))
        send[pl.ds(4 * per + part, GROUP, stride=to_each), :] = last


def forward(nodes, got, across, along, turn, send):
    cols = got.shape[1]
    per = (got.shape[0] // GROUP - 2) // 4
    group, place = place_of(nodes) // GROUP, place_of(nodes) % GROUP

    def slot(s):
        return got[pl.ds(s, GROUP, stride=4 * per + 2), :]

    real = [slot(t) for t in range(per)] + [slot(2 * per + t) for t in range(per)] + [slot(4 * per)]
    imag = [slot(per + t) for t in range(per)] + [slot(3 * per + t) for t in range(per)] + [slot(4 * per + 1)]
    both = jnp.concatenate([jnp.concatenate(real, 1), jnp.concatenate(imag, 1)], 0)
    mixed = left_dot(across[group], both, 2)
    c, s = turn[0], turn[1]
    turned = []
    for i in range(2 * per + 1):
        a = mixed[:nodes, i * cols : (i + 1) * cols]
        b = mixed[nodes:, i * cols : (i + 1) * cols]
        turned.append(jnp.concatenate([a * c + b * s, b * c - a * s], 1))
    spectrum = right_dot(jnp.concatenate(turned, 0), along[...], 2)
    kx = wavenumbers(nodes, cols)
    to_each = 2 * per + 1
    for t in range(per):
        u = spectrum[t * nodes : (t + 1) * nodes]
        g = spectrum[(per + t) * nodes : (per + t + 1) * nodes]
        send[pl.ds(t, nodes, stride=to_each), :] = g[:, :cols] - kx * u[:, cols:]
        send[pl.ds(per + t, nodes, stride=to_each), :] = g[:, cols:] + kx * u[:, :cols]
    last = spectrum[2 * per * nodes :]
    send[pl.ds(2 * per, nodes, stride=to_each), :] = jnp.where(place % 2 == 0, last[:, :cols], last[:, cols:])


def joined(first, last, a, b, c, gap):
    count, joins, span = a.shape[0], [], 1
    while span < count:

        def ahead(value, by):
            return pltpu.roll(value, count - by, 0) if by else value

        g = ahead(gap, span - 1)
        next_first, next_last = [ahead(x, span) for x in first], [ahead(x, span) for x in last]
        next_a, next_b, next_c = ahead(a, span), ahead(b, span), ahead(c, span)
        weight = g / (1.0 - g * g * c * next_a)
        by_l, by_r = b * weight, next_b * weight
        from_below = [(last[n] + c * g * next_first[n]) * weight for n in range(2)]
        from_above = [(next_first[n] + next_a * g * last[n]) * weight for n in range(2)]
        below_r, above_l = c * g * by_r, next_a * g * by_l
        joins.append(from_below + from_above + [by_l, below_r, above_l, by_r])
        first = [first[n] + b * from_above[n] for n in range(2)]
        last = [next_last[n] + next_b * from_below[n] for n in range(2)]
        a, b, c = a + b * above_l, b * by_r, next_c + next_b * below_r
        span *= 2
    return (first, last, a, b, c), joins


def parted(joins, part, lower, upper):
    run = lax.broadcasted_iota(jnp.int32, lower.shape, 0)
    for level in reversed(range(len(joins))):
        join, span = joins[level], 2**level
        later = run // span % 2 == 1
        from_below = join[part] + join[4] * lower + join[5] * upper
        from_above = join[2 + part] + join[6] * lower + join[7] * upper
        lower = jnp.where(later, pltpu.roll(from_below, span, 0), lower)
        upper = jnp.where(later, pltpu.roll(upper, span, 0), from_above)
    return lower, upper


def eliminate(nodes, got, wide, heavy, base, left, right, tree, send, rhs):
    rows, cols = wide.shape
    length = rows // SEGMENTS
    steps = lax.axis_size("gy")
    rank_x, rank_y = place_of(nodes), lax.axis_index("gy")
    per = rows // GROUP
    to_each = 2 * per + 1

    def summed(s, count):
        return sum(got[pl.ds(to_each * i + s, count, stride=to_each), :] for i in range(0, nodes, GROUP))

    for part in range(2):
        for t in range(per):
            rhs[part, pl.ds(t * GROUP, GROUP), :] = summed(part * per + t, GROUP)
    edge = [summed(2 * per + part * to_each, 1) for part in range(2)]
    place = lax.broadcasted_iota(jnp.int32, (SEGMENTS, cols), 1)
    run = lax.broadcasted_iota(jnp.int32, (SEGMENTS, cols), 0)
    kx = signed_half(rank_x + nodes * place, nodes * cols)
    square = kx * kx + KZ * KZ
    top = heavy[rows - 1 : rows, :]
    every = [pl.ds(t, SEGMENTS, stride=length) for t in range(length)]
    above = [heavy[rows_t, :] for rows_t in every]
    below = [jnp.where(run == 0, jnp.where(rank_y == 0, 0.0, STANDIN), pltpu.roll(above[-1], 1, 0))] + above[:-1]
    above[-1] = jnp.where((run == SEGMENTS - 1) & (rank_y == steps - 1), 0.0, above[-1])
    diagonal = [above[t] + below[t] + square * wide[every[t], :] for t in range(length)]
    right_side = [[rhs[part, rows_t, :] for part in range(2)] for rows_t in every]

    half = length // 2
    low, high, ratio_l, ratio_h = [], [], [], []
    for i in range(half):
        j, k = i, length - 1 - i
        if i == 0:
            inv_l, inv_h = 1.0 / diagonal[j], 1.0 / diagonal[k]
            low.append([right_side[j][0] * inv_l, right_side[j][1] * inv_l, inv_l])
            high.append([right_side[k][0] * inv_h, right_side[k][1] * inv_h, inv_h])
        else:
            gl, gh = below[j], above[k]
            inv_l = 1.0 / (diagonal[j] - gl * gl * inv_l)
            inv_h = 1.0 / (diagonal[k] - gh * gh * inv_h)
            was_l, was_h = low[-1], high[-1]
            low.append([(right_side[j][n] + gl * was_l[n]) * inv_l for n in range(2)] + [gl * was_l[2] * inv_l])
            high.append([(right_side[k][n] + gh * was_h[n]) * inv_h for n in range(2)] + [gh * was_h[2] * inv_h])
        ratio_l.append(above[j] * inv_l)
        ratio_h.append(below[k] * inv_h)
    e_l, e_h = ratio_l[-1], ratio_h[-1]
    meet = 1.0 / (1.0 - e_l * e_h)
    down = [(low[-1][n] + e_l * high[-1][n]) * meet for n in range(2)] + [low[-1][2] * meet, e_l * high[-1][2] * meet]
    up = [high[-1][n] + e_h * down[n] for n in range(2)] + [e_h * down[2], high[-1][2] + e_h * down[3]]
    for i in reversed(range(half)):
        j, k = i, length - 1 - i
        if i < half - 1:
            e_l, e_h = ratio_l[i], ratio_h[i]
            down = [low[i][n] + e_l * down[n] for n in range(3)] + [e_l * down[3]]
            up = [high[i][n] + e_h * up[n] for n in range(2)] + [e_h * up[2], high[i][2] + e_h * up[3]]
        for t, value in ((j, down), (k, up)):
            here = pl.ds(t * SEGMENTS, SEGMENTS)
            base[0, here, :], base[1, here, :], left[here, :], right[here, :] = value

    (first, last, a, b, c), joins = joined(down[:2], up[:2], down[2], down[3], up[3], above[-1])
    for level, join in enumerate(joins):
        for i, value in enumerate(join):
            tree[level, i] = value
    inv_top = 1.0 / top
    told = [x[:1] for x in first + last + [a, b, c]] + [top]
    for part in range(2):
        told[2 + part] = told[2 + part] + edge[part] * inv_top
    told = jnp.concatenate(told, 0)
    for step in range(steps):
        send[8 * step : 8 * step + 8, :] = told


def couple(nodes, steps, got, base, left, right, tree, send, chain):
    cols = left.shape[1]
    rank = lax.axis_index("gy")
    first, last, a, b, c, gap = (
        [got[pl.ds(i, steps, stride=8), :] for i in some] for some in ((0, 1), (2, 3), (4,), (5,), (6,), (7,))
    )
    a, b, c, gap = a[0], b[0], c[0], gap[0]
    block = lax.broadcasted_iota(jnp.int32, (steps, cols), 0)
    change = jnp.where(block == 0, 0.0, pltpu.roll(gap, 1, 0) - STANDIN)
    scale = 1.0 / (1.0 + a * change)
    first = [x * scale for x in first]
    last = [last[n] - b * change * first[n] for n in range(2)]
    a, b, c = a * scale, b * scale, c - b * b * change * scale
    joins = joined(first, last, a, b, c, gap)[1]
    for part in range(2):
        lower, upper = parted(joins, part, jnp.zeros_like(a), jnp.zeros_like(a))
        here = first[part] + a * lower + b * upper
        chain[3 * part] = lower - change * here
        chain[3 * part + 1] = upper
        chain[3 * part + 2] = pltpu.roll(here, steps - 1, 0)
    inner = [[tree[level, i] for i in range(8)] for level in range(LEVELS)]
    length = left.shape[0] // SEGMENTS
    per = left.shape[0] // GROUP
    to_each = 2 * per + 2
    for part in range(2):
        lower, upper, after = (chain[3 * part + i, pl.ds(rank, 1), :] for i in range(3))
        lower, upper = parted(inner, part, *(jnp.broadcast_to(x, (SEGMENTS, cols)) for x in (lower, upper)))
        for t in range(length):
            rows = pl.ds(t * SEGMENTS, SEGMENTS)
            solved = base[part, rows, :] + left[rows, :] * lower + right[rows, :] * upper
            spot = t // per * to_each + part * per + t % per
            for group in range(0, nodes, GROUP):
                send[pl.ds(group * to_each + spot, SEGMENTS, stride=length // per * to_each), :] = solved
        send[pl.ds(2 * per + part, nodes, stride=to_each), :] = jnp.broadcast_to(after, (nodes, cols))


def inverse(nodes, got, across, across_full, along, along_full, turn, send, edge, pick):
    cols = got.shape[1]
    per = got.shape[0] // nodes // 2 - 1
    group, place = place_of(nodes) // GROUP, place_of(nodes) % GROUP

    def slot(s):
        return got[pl.ds(s, nodes, stride=2 * per + 2), :]

    def turned(begun):
        c, s = turn[0], turn[1]
        real, imag = [], []
        for i in range(begun.shape[0] // nodes):
            a = begun[i * nodes : (i + 1) * nodes, :cols]
            b = begun[i * nodes : (i + 1) * nodes, cols:]
            real.append(a * c - b * s)
            imag.append(b * c + a * s)
        return jnp.concatenate([jnp.concatenate(real, 1), jnp.concatenate(imag, 1)], 0)

    kx = wavenumbers(nodes, cols)
    flow, plain = [], []
    for t in range(per):
        real, imag = slot(t), slot(per + t)
        flow.append(jnp.concatenate([-kx * imag, kx * real], 1))
        plain.append(jnp.concatenate([real, imag], 1))
    plain.append(jnp.concatenate([slot(2 * per), slot(2 * per + 1)], 1))
    plain = right_dot(jnp.concatenate(plain, 0), along_full[...], 3)
    flow = right_dot(jnp.concatenate(flow, 0), along[...], 2)
    plain = left_dot(across_full[group], turned(plain), 3)
    flow = left_dot(across[group], turned(flow), 2)
    for i, done in enumerate((flow, plain)):
        for part in range(2):
            for t in range(per):
                block = done[part * GROUP : (part + 1) * GROUP, t * cols : (t + 1) * cols]
                send[pl.ds((2 * i + part) * per + t, GROUP, stride=4 * per), :] = block
    pick[...] = plain[:, per * cols :]
    for part in range(2):
        edge[part : part + 1, :] = pick[pl.ds(place + part * GROUP, 1), :]


def finish(steps, u, v, w, got, edge, heavy, u_far, v_far, w_far, u_new, v_new, w_new, pot, left):
    rows, cols = heavy.shape
    per = rows // GROUP
    rank = lax.axis_index("gy")
    copies = [
        pltpu.make_async_copy(near.at[part], far.at[part], left.at[2 * i + part])
        for i, (near, far) in enumerate(((u_new, u_far), (w_new, w_far), (v_new, v_far)))
        for part in range(2)
    ]

    def slot(s):
        return got[pl.ds(s, GROUP, stride=4 * per), :]

    for part in range(2):
        for t in range(per):
            place = pl.ds(t, GROUP, stride=per)
            u_new[part, place, :] = u[part, place, :] - slot(part * per + t)
        copies[part].start()
    for part in range(2):
        for t in range(per):
            pot[part, pl.ds(t, GROUP, stride=per), :] = slot((2 + part) * per + t)
    for part in range(2):
        turned = KZ * pot[1 - part]
        w_new[part] = w[part] + (turned if part == 0 else -turned)
        copies[2 + part].start()
    row = lax.broadcasted_iota(jnp.int32, (rows, cols), 0)
    g = jnp.where((row == rows - 1) & (rank == steps - 1), 0.0, heavy[...])
    for part in range(2):
        here = pot[part]
        above = jnp.broadcast_to(edge[part : part + 1, :], (rows, cols))
        after = jnp.where(row == rows - 1, above, pltpu.roll(here, rows - 1, 0))
        v_new[part] = v[part] - g * (after - here)
        copies[4 + part].start()
    for copy in copies:
        copy.wait()


def call(body, outs, scratch, ins, out_spec=VMEM, semaphores=0, limit=24):
    scratch = [pltpu.VMEM(shape, F32) for shape in scratch]
    if semaphores:
        scratch.append(pltpu.SemaphoreType.DMA((semaphores,)))
    return pl.pallas_call(
        body,
        out_shape=[jax.ShapeDtypeStruct(shape, F32) for shape in outs],
        in_specs=ins,
        out_specs=[out_spec] * len(outs),
        scratch_shapes=scratch,
        compiler_params=pltpu.CompilerParams(vmem_limit_bytes=limit * 1024 * 1024),
        cost_estimate=pl.CostEstimate(flops=1000000, bytes_accessed=1000000, transcendentals=0),
    )


def exchange(array, axis, count, groups=None):
    shape = array.shape
    array = array.reshape(count, shape[0] // count * shape[1])
    return lax.all_to_all(array, axis, 0, 0, axis_index_groups=groups, tiled=True).reshape(shape)


def per_device(u_star, v_star, w_star, cell_width, face_weight):
    nodes, steps = lax.axis_size("gx"), lax.axis_size("gy")
    shape = u_star.shape
    rows, cols = shape[2:]
    wider = rows // GROUP
    across_f, across_i, across_full, along_f, along_i, along_full, turn = tables(nodes, cols)
    u, v, w = (x.reshape(2, rows, cols) for x in (u_star, v_star, w_star))
    field, plane, line = (2, rows, cols), (rows, cols), (1, rows)
    ranks = order(nodes)
    near, all_x = [ranks[i : i + GROUP] for i in range(0, nodes, GROUP)], [ranks]

    send, wide, heavy = call(
        prepare,
        [(GROUP * (4 * wider + 2), cols), plane, plane],
        [field, field, field, line, line, (4, rows, cols)],
        [HBM] * 5,
        semaphores=5,
    )(*(pltpu.with_memory_space_constraint(x, pltpu.HBM) for x in (u, v, w, cell_width.reshape(line), face_weight.reshape(line))))
    got = exchange(send, "gx", GROUP, near)
    (send,) = call(functools.partial(forward, nodes), [(nodes * (2 * wider + 1), cols)], [], [VMEM] * 4)(
        got, across_f, along_f, turn
    )
    got = exchange(send, "gx", nodes, all_x)
    base, left, right, tree, send = call(
        functools.partial(eliminate, nodes),
        [field, plane, plane, (LEVELS, 8, SEGMENTS, cols), (8 * steps, cols)],
        [field],
        [VMEM] * 3,
    )(got, wide, heavy)
    got = exchange(send, "gy", steps)
    (send,) = call(
        functools.partial(couple, nodes, steps), [(nodes * (2 * wider + 2), cols)], [(6, steps, cols)], [VMEM] * 5
    )(got, base, left, right, tree)
    got = exchange(send, "gx", nodes, all_x)
    send, edge = call(
        functools.partial(inverse, nodes), [(GROUP * 4 * wider, cols), (8, cols)], [(2 * GROUP, cols)], [VMEM] * 6
    )(got, across_i, across_full, along_i, along_full, turn)
    got = exchange(send, "gx", GROUP, near)
    outs = call(
        functools.partial(finish, steps),
        [field] * 3,
        [field] * 4,
        [VMEM] * 6,
        out_spec=HBM,
        semaphores=6,
    )(u, v, w, got, edge, heavy)
    return tuple(x.reshape(shape) for x in outs)


def solution(mesh):
    whole = P(None, None, "gy", "gx")
    return jax.shard_map(
        per_device,
        mesh=mesh,
        in_specs=(whole, whole, whole, P("gy"), P("gy")),
        out_specs=(whole, whole, whole),
        check_vma=False,
    )
```

```python
import functools
import math

import jax
import jax.numpy as jnp
import numpy as np
from jax import lax
from jax.experimental import pallas as pl
from jax.experimental.pallas import tpu as pltpu
from jax.sharding import PartitionSpec as P

FLOW_FACTOR = 0.5
SPAN_FACTOR = 1.0
KZ = SPAN_FACTOR
STANDIN = 16.0
F32 = jnp.float32
VMEM = pl.BlockSpec(memory_space=pltpu.VMEM)
HBM = pl.BlockSpec(memory_space=pltpu.HBM)
ALONG, BESIDE = 4, 4
GROUP = ALONG * BESIDE
LEVELS = 3
SEGMENTS = 2**LEVELS


OUT = [(2, 2), (1, 1), (0, 3), (1, 2), (2, 3), (3, 0), (0, 0), (0, 2), (1, 3), (2, 0), (3, 3), (2, 1), (3, 2), (1, 0), (0, 1), (3, 1)]
BACK = [(2, 2), (1, 1), (3, 0), (2, 1), (3, 2), (0, 3), (0, 0), (2, 0), (3, 1), (0, 2), (3, 3), (1, 2), (2, 3), (0, 1), (1, 0), (1, 3)]


def order(nodes, places):
    breadth = nodes // ALONG
    return [breadth * x + BESIDE * q + y for q in range(breadth // BESIDE) for x, y in places]


def place_of(nodes, places):
    rank = lax.axis_index("gx")
    return sum(jnp.where(rank == other, place, 0) for place, other in enumerate(order(nodes, places)))


def tables(nodes, cols):
    full = nodes * cols

    def cos_sin(a, b, length):
        angle = 2.0 * np.pi * (np.outer(a, b) % length) / length
        return np.cos(angle), np.sin(angle)

    ranks, residues, places = np.array(order(nodes, OUT)), np.arange(nodes), np.arange(cols)
    c, s = cos_sin(residues, ranks, nodes)
    across_f = np.stack(
        [
            np.block([[c[:, i : i + GROUP], s[:, i : i + GROUP]], [-s[:, i : i + GROUP], c[:, i : i + GROUP]]])
            for i in range(0, nodes, GROUP)
        ]
    )
    ranks = order(nodes, BACK)
    held = np.argsort(order(nodes, OUT))[ranks]
    c, s = cos_sin(np.array(ranks), held, nodes)
    across_i = np.stack(
        [
            np.block([[c[i : i + GROUP], -s[i : i + GROUP]], [s[i : i + GROUP], c[i : i + GROUP]]])
            for i in range(0, nodes, GROUP)
        ]
    )
    c, s = cos_sin(places, places, cols)
    along_f = np.block([[c, -s], [s, c]])
    along_i = np.block([[c, s], [-s, c]]) / full
    turn_f, turn_i = np.stack(cos_sin(residues, places, full)), np.stack(cos_sin(held, places, full))
    wave = held[:, None] + nodes * places
    waves = np.where(wave < full // 2, wave, wave - full) * FLOW_FACTOR
    return [
        constant_side(across_f, -1, 2),
        constant_side(across_i, -1, 2),
        constant_side(across_i, -1, 3),
        constant_side(along_f, 0, 2),
        constant_side(along_i, 0, 2),
        constant_side(along_i, 0, 3),
        *(np.asarray(x, np.float32) for x in (turn_f, turn_i, waves)),
    ]


def pairs(terms):
    return [(i, j) for i in range(terms) for j in range(terms) if i + j < terms]


def expand(value, terms, one, whole):
    parts = []
    for _ in range(terms):
        parts.append(value.astype(one))
        value = value - parts[-1].astype(whole)
    return parts


def constant_side(matrix, axis, terms):
    parts = expand(np.asarray(matrix, np.float64), terms, jnp.bfloat16, np.float64)
    return np.concatenate([parts[i] for i, _ in pairs(terms)], axis)


def data_side(value, axis, terms):
    parts = expand(value, terms, jnp.bfloat16, F32)
    return jnp.concatenate([parts[j] for _, j in pairs(terms)], axis)


def dot(a, b):
    return lax.dot_general(a, b, (((1,), (0,)), ((), ())), preferred_element_type=F32)


def left_dot(constant, value, terms):
    return dot(constant, data_side(value, 0, terms))


def right_dot(value, constant, terms):
    return dot(data_side(value, 1, terms), constant)


def signed_half(wave, full):
    return jnp.where(wave < full // 2, wave, wave - full).astype(F32) * FLOW_FACTOR


def wavenumbers(nodes, cols):
    rank = lax.broadcasted_iota(jnp.int32, (nodes, cols), 0)
    place = lax.broadcasted_iota(jnp.int32, (nodes, cols), 1)
    return signed_half(rank + nodes * place, nodes * cols)


def column(row, rows, cols):
    here = lax.broadcasted_iota(jnp.int32, (rows, rows), 0)
    there = lax.broadcasted_iota(jnp.int32, (rows, rows), 1)
    one = jnp.sum(jnp.where(here == there, jnp.broadcast_to(row, (rows, rows)), 0.0), axis=1, keepdims=True)
    return jnp.broadcast_to(one, (rows, cols))


def prepare(u_far, v_far, w_far, width_far, weight_far, send, wide, heavy, u, v, w, width, weight, tmp, arrived):
    rows, cols = u.shape[1:]
    per = rows // GROUP
    copies = [
        pltpu.make_async_copy(far, near, arrived.at[i])
        for i, (far, near) in enumerate(
            ((width_far, width), (weight_far, weight), (u_far, u), (w_far, w), (v_far, v))
        )
    ]
    for copy in copies:
        copy.start()
    copies[0].wait()
    h = column(width[...], rows, cols)
    wide[...] = h
    copies[1].wait()
    heavy[...] = column(weight[...], rows, cols)
    to_each = 4 * per + 2

    def pack(field):
        for t in range(per):
            send[pl.ds(field * per + t, GROUP, stride=to_each), :] = tmp[field, pl.ds(t * GROUP, GROUP), :]

    copies[2].wait()
    for part in range(2):
        tmp[part] = -h * u[part]
        pack(part)
    copies[3].wait()
    copies[4].wait()
    first = lax.broadcasted_iota(jnp.int32, (rows, cols), 0) == 0
    for part in range(2):
        now = v[part]
        below = jnp.where(first, 0.0, pltpu.roll(now, 1, 0))
        other = w[1 - part] * (h * KZ)
        tmp[2 + part] = below - now + (other if part == 0 else -other)
        pack(2 + part)
        last = jnp.broadcast_to(v[part, rows - 1 : rows, :], (GROUP, cols))
        send[pl.ds(4 * per + part, GROUP, stride=to_each), :] = last


def forward(nodes, got, across, along, turn, send):
    cols = got.shape[1]
    per = (got.shape[0] // GROUP - 2) // 4
    group, place = place_of(nodes, OUT) // GROUP, place_of(nodes, OUT) % GROUP

    def slot(s):
        return got[pl.ds(s, GROUP, stride=4 * per + 2), :]

    real = [slot(t) for t in range(per)] + [slot(2 * per + t) for t in range(per)] + [slot(4 * per)]
    imag = [slot(per + t) for t in range(per)] + [slot(3 * per + t) for t in range(per)] + [slot(4 * per + 1)]
    both = jnp.concatenate([jnp.concatenate(real, 1), jnp.concatenate(imag, 1)], 0)
    mixed = left_dot(across[group], both, 2)
    c, s = turn[0], turn[1]
    turned = []
    for i in range(2 * per + 1):
        a = mixed[:nodes, i * cols : (i + 1) * cols]
        b = mixed[nodes:, i * cols : (i + 1) * cols]
        turned.append(jnp.concatenate([a * c + b * s, b * c - a * s], 1))
    spectrum = right_dot(jnp.concatenate(turned, 0), along[...], 2)
    kx = wavenumbers(nodes, cols)
    to_each = 2 * per + 1
    for t in range(per):
        u = spectrum[t * nodes : (t + 1) * nodes]
        g = spectrum[(per + t) * nodes : (per + t + 1) * nodes]
        send[pl.ds(t, nodes, stride=to_each), :] = g[:, :cols] - kx * u[:, cols:]
        send[pl.ds(per + t, nodes, stride=to_each), :] = g[:, cols:] + kx * u[:, :cols]
    last = spectrum[2 * per * nodes :]
    send[pl.ds(2 * per, nodes, stride=to_each), :] = jnp.where(place % 2 == 0, last[:, :cols], last[:, cols:])


def joined(first, last, a, b, c, gap):
    count, joins, span = a.shape[0], [], 1
    while span < count:

        def ahead(value, by):
            return pltpu.roll(value, count - by, 0) if by else value

        g = ahead(gap, span - 1)
        next_first, next_last = [ahead(x, span) for x in first], [ahead(x, span) for x in last]
        next_a, next_b, next_c = ahead(a, span), ahead(b, span), ahead(c, span)
        weight = g / (1.0 - g * g * c * next_a)
        by_l, by_r = b * weight, next_b * weight
        from_below = [(last[n] + c * g * next_first[n]) * weight for n in range(2)]
        from_above = [(next_first[n] + next_a * g * last[n]) * weight for n in range(2)]
        below_r, above_l = c * g * by_r, next_a * g * by_l
        joins.append(from_below + from_above + [by_l, below_r, above_l, by_r])
        first = [first[n] + b * from_above[n] for n in range(2)]
        last = [next_last[n] + next_b * from_below[n] for n in range(2)]
        a, b, c = a + b * above_l, b * by_r, next_c + next_b * below_r
        span *= 2
    return (first, last, a, b, c), joins


def parted(joins, part, lower, upper):
    run = lax.broadcasted_iota(jnp.int32, lower.shape, 0)
    for level in reversed(range(len(joins))):
        join, span = joins[level], 2**level
        later = run // span % 2 == 1
        from_below = join[part] + join[4] * lower + join[5] * upper
        from_above = join[2 + part] + join[6] * lower + join[7] * upper
        lower = jnp.where(later, pltpu.roll(from_below, span, 0), lower)
        upper = jnp.where(later, pltpu.roll(upper, span, 0), from_above)
    return lower, upper


def eliminate(nodes, got, wide, heavy, base, left, right, tree, send, rhs):
    rows, cols = wide.shape
    length = rows // SEGMENTS
    steps = lax.axis_size("gy")
    rank_x, rank_y = place_of(nodes, OUT), lax.axis_index("gy")
    per = rows // GROUP
    to_each = 2 * per + 1

    def summed(s, count):
        return sum(got[pl.ds(to_each * i + s, count, stride=to_each), :] for i in range(0, nodes, GROUP))

    for part in range(2):
        for t in range(per):
            rhs[part, pl.ds(t * GROUP, GROUP), :] = summed(part * per + t, GROUP)
    edge = [summed(2 * per + part * to_each, 1) for part in range(2)]
    place = lax.broadcasted_iota(jnp.int32, (SEGMENTS, cols), 1)
    run = lax.broadcasted_iota(jnp.int32, (SEGMENTS, cols), 0)
    kx = signed_half(rank_x + nodes * place, nodes * cols)
    square = kx * kx + KZ * KZ
    top = heavy[rows - 1 : rows, :]
    every = [pl.ds(t, SEGMENTS, stride=length) for t in range(length)]
    above = [heavy[rows_t, :] for rows_t in every]
    below = [jnp.where(run == 0, jnp.where(rank_y == 0, 0.0, STANDIN), pltpu.roll(above[-1], 1, 0))] + above[:-1]
    above[-1] = jnp.where((run == SEGMENTS - 1) & (rank_y == steps - 1), 0.0, above[-1])
    diagonal = [above[t] + below[t] + square * wide[every[t], :] for t in range(length)]
    right_side = [[rhs[part, rows_t, :] for part in range(2)] for rows_t in every]

    half = length // 2
    low, high, ratio_l, ratio_h = [], [], [], []
    for i in range(half):
        j, k = i, length - 1 - i
        if i == 0:
            inv_l, inv_h = 1.0 / diagonal[j], 1.0 / diagonal[k]
            low.append([right_side[j][0] * inv_l, right_side[j][1] * inv_l, inv_l])
            high.append([right_side[k][0] * inv_h, right_side[k][1] * inv_h, inv_h])
        else:
            gl, gh = below[j], above[k]
            inv_l = 1.0 / (diagonal[j] - gl * gl * inv_l)
            inv_h = 1.0 / (diagonal[k] - gh * gh * inv_h)
            was_l, was_h = low[-1], high[-1]
            low.append([(right_side[j][n] + gl * was_l[n]) * inv_l for n in range(2)] + [gl * was_l[2] * inv_l])
            high.append([(right_side[k][n] + gh * was_h[n]) * inv_h for n in range(2)] + [gh * was_h[2] * inv_h])
        ratio_l.append(above[j] * inv_l)
        ratio_h.append(below[k] * inv_h)
    e_l, e_h = ratio_l[-1], ratio_h[-1]
    meet = 1.0 / (1.0 - e_l * e_h)
    down = [(low[-1][n] + e_l * high[-1][n]) * meet for n in range(2)] + [low[-1][2] * meet, e_l * high[-1][2] * meet]
    up = [high[-1][n] + e_h * down[n] for n in range(2)] + [e_h * down[2], high[-1][2] + e_h * down[3]]
    for i in reversed(range(half)):
        j, k = i, length - 1 - i
        if i < half - 1:
            e_l, e_h = ratio_l[i], ratio_h[i]
            down = [low[i][n] + e_l * down[n] for n in range(3)] + [e_l * down[3]]
            up = [high[i][n] + e_h * up[n] for n in range(2)] + [e_h * up[2], high[i][2] + e_h * up[3]]
        for t, value in ((j, down), (k, up)):
            here = pl.ds(t * SEGMENTS, SEGMENTS)
            base[0, here, :], base[1, here, :], left[here, :], right[here, :] = value

    (first, last, a, b, c), joins = joined(down[:2], up[:2], down[2], down[3], up[3], above[-1])
    for level, join in enumerate(joins):
        for i, value in enumerate(join):
            tree[level, i] = value
    inv_top = 1.0 / top
    told = [x[:1] for x in first + last + [a, b, c]] + [top]
    for part in range(2):
        told[2 + part] = told[2 + part] + edge[part] * inv_top
    told = jnp.concatenate(told, 0)
    for step in range(steps):
        send[8 * step : 8 * step + 8, :] = told


def couple(nodes, steps, got, base, left, right, tree, send, chain):
    cols = left.shape[1]
    rank = lax.axis_index("gy")
    first, last, a, b, c, gap = (
        [got[pl.ds(i, steps, stride=8), :] for i in some] for some in ((0, 1), (2, 3), (4,), (5,), (6,), (7,))
    )
    a, b, c, gap = a[0], b[0], c[0], gap[0]
    block = lax.broadcasted_iota(jnp.int32, (steps, cols), 0)
    change = jnp.where(block == 0, 0.0, pltpu.roll(gap, 1, 0) - STANDIN)
    scale = 1.0 / (1.0 + a * change)
    first = [x * scale for x in first]
    last = [last[n] - b * change * first[n] for n in range(2)]
    a, b, c = a * scale, b * scale, c - b * b * change * scale
    joins = joined(first, last, a, b, c, gap)[1]
    for part in range(2):
        lower, upper = parted(joins, part, jnp.zeros_like(a), jnp.zeros_like(a))
        here = first[part] + a * lower + b * upper
        chain[3 * part] = lower - change * here
        chain[3 * part + 1] = upper
        chain[3 * part + 2] = pltpu.roll(here, steps - 1, 0)
    inner = [[tree[level, i] for i in range(8)] for level in range(LEVELS)]
    length = left.shape[0] // SEGMENTS
    per = left.shape[0] // GROUP
    to_each = 2 * per + 2
    for part in range(2):
        lower, upper, after = (chain[3 * part + i, pl.ds(rank, 1), :] for i in range(3))
        lower, upper = parted(inner, part, *(jnp.broadcast_to(x, (SEGMENTS, cols)) for x in (lower, upper)))
        for t in range(length):
            rows = pl.ds(t * SEGMENTS, SEGMENTS)
            solved = base[part, rows, :] + left[rows, :] * lower + right[rows, :] * upper
            spot = t // per * to_each + part * per + t % per
            for group in range(0, nodes, GROUP):
                send[pl.ds(group * to_each + spot, SEGMENTS, stride=length // per * to_each), :] = solved
        send[pl.ds(2 * per + part, nodes, stride=to_each), :] = jnp.broadcast_to(after, (nodes, cols))


def inverse(nodes, got, across, across_full, along, along_full, turn, waves, send, edge, pick):
    cols = got.shape[1]
    per = got.shape[0] // nodes // 2 - 1
    group, place = place_of(nodes, BACK) // GROUP, place_of(nodes, BACK) % GROUP

    def slot(s):
        return got[pl.ds(s, nodes, stride=2 * per + 2), :]

    def turned(begun):
        c, s = turn[0], turn[1]
        real, imag = [], []
        for i in range(begun.shape[0] // nodes):
            a = begun[i * nodes : (i + 1) * nodes, :cols]
            b = begun[i * nodes : (i + 1) * nodes, cols:]
            real.append(a * c - b * s)
            imag.append(b * c + a * s)
        return jnp.concatenate([jnp.concatenate(real, 1), jnp.concatenate(imag, 1)], 0)

    kx = waves[...]
    flow, plain = [], []
    for t in range(per):
        real, imag = slot(t), slot(per + t)
        flow.append(jnp.concatenate([-kx * imag, kx * real], 1))
        plain.append(jnp.concatenate([real, imag], 1))
    plain.append(jnp.concatenate([slot(2 * per), slot(2 * per + 1)], 1))
    plain = right_dot(jnp.concatenate(plain, 0), along_full[...], 3)
    flow = right_dot(jnp.concatenate(flow, 0), along[...], 2)
    plain = left_dot(across_full[group], turned(plain), 3)
    flow = left_dot(across[group], turned(flow), 2)
    for i, done in enumerate((flow, plain)):
        for part in range(2):
            for t in range(per):
                block = done[part * GROUP : (part + 1) * GROUP, t * cols : (t + 1) * cols]
                send[pl.ds((2 * i + part) * per + t, GROUP, stride=4 * per), :] = block
    pick[...] = plain[:, per * cols :]
    for part in range(2):
        edge[part : part + 1, :] = pick[pl.ds(place + part * GROUP, 1), :]


def finish(steps, u, v, w, got, edge, heavy, u_far, v_far, w_far, u_new, v_new, w_new, pot, left):
    rows, cols = heavy.shape
    per = rows // GROUP
    rank = lax.axis_index("gy")
    copies = [
        pltpu.make_async_copy(near.at[part], far.at[part], left.at[2 * i + part])
        for i, (near, far) in enumerate(((u_new, u_far), (w_new, w_far), (v_new, v_far)))
        for part in range(2)
    ]

    def slot(s):
        return got[pl.ds(s, GROUP, stride=4 * per), :]

    for part in range(2):
        for t in range(per):
            place = pl.ds(t, GROUP, stride=per)
            u_new[part, place, :] = u[part, place, :] - slot(part * per + t)
        copies[part].start()
    for part in range(2):
        for t in range(per):
            pot[part, pl.ds(t, GROUP, stride=per), :] = slot((2 + part) * per + t)
    for part in range(2):
        turned = KZ * pot[1 - part]
        w_new[part] = w[part] + (turned if part == 0 else -turned)
        copies[2 + part].start()
    row = lax.broadcasted_iota(jnp.int32, (rows, cols), 0)
    g = jnp.where((row == rows - 1) & (rank == steps - 1), 0.0, heavy[...])
    for part in range(2):
        here = pot[part]
        above = jnp.broadcast_to(edge[part : part + 1, :], (rows, cols))
        after = jnp.where(row == rows - 1, above, pltpu.roll(here, rows - 1, 0))
        v_new[part] = v[part] - g * (after - here)
        copies[4 + part].start()
    for copy in copies:
        copy.wait()


def call(body, outs, scratch, ins, out_spec=VMEM, semaphores=0, limit=24):
    scratch = [pltpu.VMEM(shape, F32) for shape in scratch]
    if semaphores:
        scratch.append(pltpu.SemaphoreType.DMA((semaphores,)))
    return pl.pallas_call(
        body,
        out_shape=[jax.ShapeDtypeStruct(shape, F32) for shape in outs],
        in_specs=ins,
        out_specs=[out_spec] * len(outs),
        scratch_shapes=scratch,
        compiler_params=pltpu.CompilerParams(vmem_limit_bytes=limit * 1024 * 1024),
        cost_estimate=pl.CostEstimate(flops=1000000, bytes_accessed=1000000, transcendentals=0),
    )


def exchange(array, axis, count, groups=None):
    shape = array.shape
    array = array.reshape(count, shape[0] // count * shape[1])
    return lax.all_to_all(array, axis, 0, 0, axis_index_groups=groups, tiled=True).reshape(shape)


def per_device(u_star, v_star, w_star, cell_width, face_weight):
    nodes, steps = lax.axis_size("gx"), lax.axis_size("gy")
    shape = u_star.shape
    rows, cols = shape[2:]
    wider = rows // GROUP
    across_f, across_i, across_full, along_f, along_i, along_full, turn_f, turn_i, waves = tables(nodes, cols)
    u, v, w = (x.reshape(2, rows, cols) for x in (u_star, v_star, w_star))
    field, plane, line = (2, rows, cols), (rows, cols), (1, rows)
    (near_out, all_out), (near_back, all_back) = (
        ([ranks[i : i + GROUP] for i in range(0, nodes, GROUP)], [ranks])
        for ranks in (order(nodes, OUT), order(nodes, BACK))
    )

    send, wide, heavy = call(
        prepare,
        [(GROUP * (4 * wider + 2), cols), plane, plane],
        [field, field, field, line, line, (4, rows, cols)],
        [HBM] * 5,
        semaphores=5,
    )(*(pltpu.with_memory_space_constraint(x, pltpu.HBM) for x in (u, v, w, cell_width.reshape(line), face_weight.reshape(line))))
    got = exchange(send, "gx", GROUP, near_out)
    (send,) = call(functools.partial(forward, nodes), [(nodes * (2 * wider + 1), cols)], [], [VMEM] * 4)(
        got, across_f, along_f, turn_f
    )
    got = exchange(send, "gx", nodes, all_out)
    base, left, right, tree, send = call(
        functools.partial(eliminate, nodes),
        [field, plane, plane, (LEVELS, 8, SEGMENTS, cols), (8 * steps, cols)],
        [field],
        [VMEM] * 3,
    )(got, wide, heavy)
    got = exchange(send, "gy", steps)
    (send,) = call(
        functools.partial(couple, nodes, steps), [(nodes * (2 * wider + 2), cols)], [(6, steps, cols)], [VMEM] * 5
    )(got, base, left, right, tree)
    got = exchange(send, "gx", nodes, all_back)
    send, edge = call(
        functools.partial(inverse, nodes), [(GROUP * 4 * wider, cols), (8, cols)], [(2 * GROUP, cols)], [VMEM] * 7
    )(got, across_i, across_full, along_i, along_full, turn_i, waves)
    got = exchange(send, "gx", GROUP, near_back)
    outs = call(
        functools.partial(finish, steps),
        [field] * 3,
        [field] * 4,
        [VMEM] * 6,
        out_spec=HBM,
        semaphores=6,
    )(u, v, w, got, edge, heavy)
    return tuple(x.reshape(shape) for x in outs)


def solution(mesh):
    whole = P(None, None, "gy", "gx")
    return jax.shard_map(
        per_device,
        mesh=mesh,
        in_specs=(whole, whole, whole, P("gy"), P("gy")),
        out_specs=(whole, whole, whole),
        check_vma=False,
    )
```

```python
import functools
import math

import jax
import jax.numpy as jnp
import numpy as np
from jax import lax
from jax.experimental import pallas as pl
from jax.experimental.pallas import tpu as pltpu
from jax.sharding import PartitionSpec as P

FLOW_FACTOR = 0.5
SPAN_FACTOR = 1.0
KZ = SPAN_FACTOR
STANDIN = 16.0
F32 = jnp.float32
VMEM = pl.BlockSpec(memory_space=pltpu.VMEM)
HBM = pl.BlockSpec(memory_space=pltpu.HBM)
ALONG, BESIDE = 4, 4
GROUP = ALONG * BESIDE
LEVELS = 3
SEGMENTS = 2**LEVELS


OUT = [(2, 2), (1, 1), (0, 3), (1, 2), (2, 3), (3, 0), (0, 0), (0, 2), (1, 3), (2, 0), (3, 3), (2, 1), (3, 2), (1, 0), (0, 1), (3, 1)]
BACK = [(2, 2), (1, 1), (3, 0), (2, 1), (3, 2), (0, 3), (0, 0), (2, 0), (3, 1), (0, 2), (3, 3), (1, 2), (2, 3), (0, 1), (1, 0), (1, 3)]


def order(nodes, places):
    breadth = nodes // ALONG
    return [breadth * x + BESIDE * q + y for q in range(breadth // BESIDE) for x, y in places]


def place_of(nodes, places):
    rank = lax.axis_index("gx")
    return sum(jnp.where(rank == other, place, 0) for place, other in enumerate(order(nodes, places)))


def tables(nodes, cols):
    full = nodes * cols

    def cos_sin(a, b, length):
        angle = 2.0 * np.pi * (np.outer(a, b) % length) / length
        return np.cos(angle), np.sin(angle)

    ranks, residues, places = np.array(order(nodes, OUT)), np.arange(nodes), np.arange(cols)
    c, s = cos_sin(residues, ranks, nodes)
    across_f = np.stack(
        [
            np.block([[c[:, i : i + GROUP], s[:, i : i + GROUP]], [-s[:, i : i + GROUP], c[:, i : i + GROUP]]])
            for i in range(0, nodes, GROUP)
        ]
    )
    ranks = order(nodes, BACK)
    held = np.argsort(order(nodes, OUT))[ranks]
    c, s = cos_sin(np.array(ranks), held, nodes)
    across_i = np.stack(
        [
            np.block([[c[i : i + GROUP], -s[i : i + GROUP]], [s[i : i + GROUP], c[i : i + GROUP]]])
            for i in range(0, nodes, GROUP)
        ]
    )
    c, s = cos_sin(places, places, cols)
    along_f = np.block([[c, -s], [s, c]])
    along_i = np.block([[c, s], [-s, c]]) / full
    turn_f, turn_i = np.stack(cos_sin(residues, places, full)), np.stack(cos_sin(held, places, full))
    wave = held[:, None] + nodes * places
    waves = np.where(wave < full // 2, wave, wave - full) * FLOW_FACTOR
    return [
        constant_side(across_f, -1, 2),
        constant_side(across_i, -1, 2),
        constant_side(across_i, -1, 3),
        constant_side(along_f, 0, 2),
        constant_side(along_i, 0, 2),
        constant_side(along_i, 0, 3),
        *(np.asarray(x, np.float32) for x in (turn_f, turn_i, waves)),
    ]


def pairs(terms):
    return [(i, j) for i in range(terms) for j in range(terms) if i + j < terms]


def expand(value, terms, one, whole):
    parts = []
    for _ in range(terms):
        parts.append(value.astype(one))
        value = value - parts[-1].astype(whole)
    return parts


def constant_side(matrix, axis, terms):
    parts = expand(np.asarray(matrix, np.float64), terms, jnp.bfloat16, np.float64)
    return np.concatenate([parts[i] for i, _ in pairs(terms)], axis)


def data_side(value, axis, terms):
    parts = expand(value, terms, jnp.bfloat16, F32)
    return jnp.concatenate([parts[j] for _, j in pairs(terms)], axis)


def dot(a, b):
    return lax.dot_general(a, b, (((1,), (0,)), ((), ())), preferred_element_type=F32)


def left_dot(constant, value, terms):
    return dot(constant, data_side(value, 0, terms))


def right_dot(value, constant, terms):
    return dot(data_side(value, 1, terms), constant)


def signed_half(wave, full):
    return jnp.where(wave < full // 2, wave, wave - full).astype(F32) * FLOW_FACTOR


def wavenumbers(nodes, cols):
    rank = lax.broadcasted_iota(jnp.int32, (nodes, cols), 0)
    place = lax.broadcasted_iota(jnp.int32, (nodes, cols), 1)
    return signed_half(rank + nodes * place, nodes * cols)


def column(row, rows, cols):
    here = lax.broadcasted_iota(jnp.int32, (rows, rows), 0)
    there = lax.broadcasted_iota(jnp.int32, (rows, rows), 1)
    one = jnp.sum(jnp.where(here == there, jnp.broadcast_to(row, (rows, rows)), 0.0), axis=1, keepdims=True)
    return jnp.broadcast_to(one, (rows, cols))


def prepare(u_far, v_far, w_far, width_far, weight_far, send, wide, heavy, u, v, w, width, weight, tmp, arrived):
    rows, cols = u.shape[1:]
    per = rows // GROUP
    copies = [
        pltpu.make_async_copy(far, near, arrived.at[i])
        for i, (far, near) in enumerate(
            ((width_far, width), (weight_far, weight), (u_far, u), (w_far, w), (v_far, v))
        )
    ]
    for copy in copies:
        copy.start()
    copies[0].wait()
    h = column(width[...], rows, cols)
    wide[...] = h
    copies[1].wait()
    heavy[...] = column(weight[...], rows, cols)
    to_each = 4 * per + 2

    def pack(field):
        for t in range(per):
            send[pl.ds(field * per + t, GROUP, stride=to_each), :] = tmp[field, pl.ds(t * GROUP, GROUP), :]

    copies[2].wait()
    for part in range(2):
        tmp[part] = -h * u[part]
        pack(part)
    copies[3].wait()
    copies[4].wait()
    first = lax.broadcasted_iota(jnp.int32, (rows, cols), 0) == 0
    for part in range(2):
        now = v[part]
        below = jnp.where(first, 0.0, pltpu.roll(now, 1, 0))
        other = w[1 - part] * (h * KZ)
        tmp[2 + part] = below - now + (other if part == 0 else -other)
        pack(2 + part)
        last = jnp.broadcast_to(v[part, rows - 1 : rows, :], (GROUP, cols))
        send[pl.ds(4 * per + part, GROUP, stride=to_each), :] = last


def forward(nodes, got, across, along, turn, send):
    cols = got.shape[1]
    per = (got.shape[0] // GROUP - 2) // 4
    group, place = place_of(nodes, OUT) // GROUP, place_of(nodes, OUT) % GROUP

    def slot(s):
        return got[pl.ds(s, GROUP, stride=4 * per + 2), :]

    real = [slot(t) for t in range(per)] + [slot(2 * per + t) for t in range(per)] + [slot(4 * per)]
    imag = [slot(per + t) for t in range(per)] + [slot(3 * per + t) for t in range(per)] + [slot(4 * per + 1)]
    both = jnp.concatenate([jnp.concatenate(real, 1), jnp.concatenate(imag, 1)], 0)
    mixed = left_dot(across[group], both, 2)
    c, s = turn[0], turn[1]
    turned = []
    for i in range(2 * per + 1):
        a = mixed[:nodes, i * cols : (i + 1) * cols]
        b = mixed[nodes:, i * cols : (i + 1) * cols]
        turned.append(jnp.concatenate([a * c + b * s, b * c - a * s], 1))
    spectrum = right_dot(jnp.concatenate(turned, 0), along[...], 2)
    kx = wavenumbers(nodes, cols)
    to_each = 2 * per + 1
    for t in range(per):
        u = spectrum[t * nodes : (t + 1) * nodes]
        g = spectrum[(per + t) * nodes : (per + t + 1) * nodes]
        send[pl.ds(t, nodes, stride=to_each), :] = g[:, :cols] - kx * u[:, cols:]
        send[pl.ds(per + t, nodes, stride=to_each), :] = g[:, cols:] + kx * u[:, :cols]
    last = spectrum[2 * per * nodes :]
    send[pl.ds(2 * per, nodes, stride=to_each), :] = jnp.where(place % 2 == 0, last[:, :cols], last[:, cols:])


def joined(first, last, a, b, c, gap):
    count, joins, span = a.shape[0], [], 1
    while span < count:

        def ahead(value, by):
            return pltpu.roll(value, count - by, 0) if by else value

        g = ahead(gap, span - 1)
        next_first, next_last = [ahead(x, span) for x in first], [ahead(x, span) for x in last]
        next_a, next_b, next_c = ahead(a, span), ahead(b, span), ahead(c, span)
        weight = g / (1.0 - g * g * c * next_a)
        by_l, by_r = b * weight, next_b * weight
        from_below = [(last[n] + c * g * next_first[n]) * weight for n in range(2)]
        from_above = [(next_first[n] + next_a * g * last[n]) * weight for n in range(2)]
        below_r, above_l = c * g * by_r, next_a * g * by_l
        joins.append(from_below + from_above + [by_l, below_r, above_l, by_r])
        first = [first[n] + b * from_above[n] for n in range(2)]
        last = [next_last[n] + next_b * from_below[n] for n in range(2)]
        a, b, c = a + b * above_l, b * by_r, next_c + next_b * below_r
        span *= 2
    return (first, last, a, b, c), joins


def parted(joins, part, lower, upper):
    run = lax.broadcasted_iota(jnp.int32, lower.shape, 0)
    for level in reversed(range(len(joins))):
        join, span = joins[level], 2**level
        later = run // span % 2 == 1
        from_below = join[part] + join[4] * lower + join[5] * upper
        from_above = join[2 + part] + join[6] * lower + join[7] * upper
        lower = jnp.where(later, pltpu.roll(from_below, span, 0), lower)
        upper = jnp.where(later, pltpu.roll(upper, span, 0), from_above)
    return lower, upper


def eliminate(nodes, got, wide, heavy, base, left, right, tree, send, rhs):
    rows, cols = wide.shape
    length = rows // SEGMENTS
    steps = lax.axis_size("gy")
    rank_x, rank_y = place_of(nodes, OUT), lax.axis_index("gy")
    per = rows // GROUP
    to_each = 2 * per + 1

    def summed(s, count):
        return sum(got[pl.ds(to_each * i + s, count, stride=to_each), :] for i in range(0, nodes, GROUP))

    for part in range(2):
        for t in range(per):
            rhs[part, pl.ds(t * GROUP, GROUP), :] = summed(part * per + t, GROUP)
    edge = [summed(2 * per + part * to_each, 1) for part in range(2)]
    place = lax.broadcasted_iota(jnp.int32, (SEGMENTS, cols), 1)
    run = lax.broadcasted_iota(jnp.int32, (SEGMENTS, cols), 0)
    kx = signed_half(rank_x + nodes * place, nodes * cols)
    square = kx * kx + KZ * KZ
    top = heavy[rows - 1 : rows, :]
    every = [pl.ds(t, SEGMENTS, stride=length) for t in range(length)]
    above = [heavy[rows_t, :] for rows_t in every]
    below = [jnp.where(run == 0, jnp.where(rank_y == 0, 0.0, STANDIN), pltpu.roll(above[-1], 1, 0))] + above[:-1]
    above[-1] = jnp.where((run == SEGMENTS - 1) & (rank_y == steps - 1), 0.0, above[-1])
    diagonal = [above[t] + below[t] + square * wide[every[t], :] for t in range(length)]
    right_side = [[rhs[part, rows_t, :] for part in range(2)] for rows_t in every]

    half = length // 2
    low, high, ratio_l, ratio_h = [], [], [], []
    for i in range(half):
        j, k = i, length - 1 - i
        if i == 0:
            inv_l, inv_h = 1.0 / diagonal[j], 1.0 / diagonal[k]
            low.append([right_side[j][0] * inv_l, right_side[j][1] * inv_l, inv_l])
            high.append([right_side[k][0] * inv_h, right_side[k][1] * inv_h, inv_h])
        else:
            gl, gh = below[j], above[k]
            inv_l = 1.0 / (diagonal[j] - gl * gl * inv_l)
            inv_h = 1.0 / (diagonal[k] - gh * gh * inv_h)
            was_l, was_h = low[-1], high[-1]
            low.append([(right_side[j][n] + gl * was_l[n]) * inv_l for n in range(2)] + [gl * was_l[2] * inv_l])
            high.append([(right_side[k][n] + gh * was_h[n]) * inv_h for n in range(2)] + [gh * was_h[2] * inv_h])
        ratio_l.append(above[j] * inv_l)
        ratio_h.append(below[k] * inv_h)
    e_l, e_h = ratio_l[-1], ratio_h[-1]
    meet = 1.0 / (1.0 - e_l * e_h)
    down = [(low[-1][n] + e_l * high[-1][n]) * meet for n in range(2)] + [low[-1][2] * meet, e_l * high[-1][2] * meet]
    up = [high[-1][n] + e_h * down[n] for n in range(2)] + [e_h * down[2], high[-1][2] + e_h * down[3]]
    for i in reversed(range(half)):
        j, k = i, length - 1 - i
        if i < half - 1:
            e_l, e_h = ratio_l[i], ratio_h[i]
            down = [low[i][n] + e_l * down[n] for n in range(3)] + [e_l * down[3]]
            up = [high[i][n] + e_h * up[n] for n in range(2)] + [e_h * up[2], high[i][2] + e_h * up[3]]
        for t, value in ((j, down), (k, up)):
            here = pl.ds(t * SEGMENTS, SEGMENTS)
            base[0, here, :], base[1, here, :], left[here, :], right[here, :] = value

    (first, last, a, b, c), joins = joined(down[:2], up[:2], down[2], down[3], up[3], above[-1])
    for level, join in enumerate(joins):
        for i, value in enumerate(join):
            tree[level, i] = value
    inv_top = 1.0 / top
    told = [x[:1] for x in first + last + [a, b, c]] + [top]
    for part in range(2):
        told[2 + part] = told[2 + part] + edge[part] * inv_top
    told = jnp.concatenate(told, 0)
    for step in range(steps):
        send[8 * step : 8 * step + 8, :] = told


def couple(nodes, steps, got, base, left, right, tree, send, chain):
    cols = left.shape[1]
    rank = lax.axis_index("gy")
    first, last, a, b, c, gap = (
        [got[pl.ds(i, steps, stride=8), :] for i in some] for some in ((0, 1), (2, 3), (4,), (5,), (6,), (7,))
    )
    a, b, c, gap = a[0], b[0], c[0], gap[0]
    block = lax.broadcasted_iota(jnp.int32, (steps, cols), 0)
    change = jnp.where(block == 0, 0.0, pltpu.roll(gap, 1, 0) - STANDIN)
    scale = 1.0 / (1.0 + a * change)
    first = [x * scale for x in first]
    last = [last[n] - b * change * first[n] for n in range(2)]
    a, b, c = a * scale, b * scale, c - b * b * change * scale
    joins = joined(first, last, a, b, c, gap)[1]
    for part in range(2):
        lower, upper = parted(joins, part, jnp.zeros_like(a), jnp.zeros_like(a))
        here = first[part] + a * lower + b * upper
        chain[3 * part] = lower - change * here
        chain[3 * part + 1] = upper
        chain[3 * part + 2] = pltpu.roll(here, steps - 1, 0)
    inner = [[tree[level, i] for i in range(8)] for level in range(LEVELS)]
    length = left.shape[0] // SEGMENTS
    per = left.shape[0] // GROUP
    to_each = 2 * per + 2
    for part in range(2):
        lower, upper, after = (chain[3 * part + i, pl.ds(rank, 1), :] for i in range(3))
        lower, upper = parted(inner, part, *(jnp.broadcast_to(x, (SEGMENTS, cols)) for x in (lower, upper)))
        for t in range(length):
            rows = pl.ds(t * SEGMENTS, SEGMENTS)
            solved = base[part, rows, :] + left[rows, :] * lower + right[rows, :] * upper
            spot = t // per * to_each + part * per + t % per
            for group in range(0, nodes, GROUP):
                send[pl.ds(group * to_each + spot, SEGMENTS, stride=length // per * to_each), :] = solved
        send[pl.ds(2 * per + part, nodes, stride=to_each), :] = jnp.broadcast_to(after, (nodes, cols))


def inverse(nodes, got, across, across_full, along, along_full, turn, waves, send, edge, pick):
    cols = got.shape[1]
    per = got.shape[0] // nodes // 2 - 1
    group, place = place_of(nodes, BACK) // GROUP, place_of(nodes, BACK) % GROUP

    def slot(s):
        return got[pl.ds(s, nodes, stride=2 * per + 2), :]

    def turned(begun):
        c, s = turn[0], turn[1]
        real, imag = [], []
        for i in range(begun.shape[0] // nodes):
            a = begun[i * nodes : (i + 1) * nodes, :cols]
            b = begun[i * nodes : (i + 1) * nodes, cols:]
            real.append(a * c - b * s)
            imag.append(b * c + a * s)
        return jnp.concatenate([jnp.concatenate(real, 1), jnp.concatenate(imag, 1)], 0)

    kx = waves[...]
    flow, plain = [], []
    for t in range(per):
        real, imag = slot(t), slot(per + t)
        flow.append(jnp.concatenate([-kx * imag, kx * real], 1))
        plain.append(jnp.concatenate([real, imag], 1))
    plain.append(jnp.concatenate([slot(2 * per), slot(2 * per + 1)], 1))
    flow = right_dot(jnp.concatenate(flow, 0), along[...], 2)
    plain = right_dot(jnp.concatenate(plain, 0), along_full[...], 3)
    flow = left_dot(across[group], turned(flow), 2)
    plain = left_dot(across_full[group], turned(plain), 3)
    for i, done in enumerate((flow, plain)):
        for part in range(2):
            for t in range(per):
                block = done[part * GROUP : (part + 1) * GROUP, t * cols : (t + 1) * cols]
                send[pl.ds((2 * i + part) * per + t, GROUP, stride=4 * per), :] = block
    pick[...] = plain[:, per * cols :]
    for part in range(2):
        edge[part : part + 1, :] = pick[pl.ds(place + part * GROUP, 1), :]


def finish(steps, u, v, w, got, edge, heavy, u_far, v_far, w_far, u_new, v_new, w_new, pot, left):
    rows, cols = heavy.shape
    per = rows // GROUP
    rank = lax.axis_index("gy")
    copies = [
        pltpu.make_async_copy(near.at[part], far.at[part], left.at[2 * i + part])
        for i, (near, far) in enumerate(((u_new, u_far), (w_new, w_far), (v_new, v_far)))
        for part in range(2)
    ]

    def slot(s):
        return got[pl.ds(s, GROUP, stride=4 * per), :]

    for part in range(2):
        for t in range(per):
            place = pl.ds(t, GROUP, stride=per)
            u_new[part, place, :] = u[part, place, :] - slot(part * per + t)
        copies[part].start()
    for part in range(2):
        for t in range(per):
            pot[part, pl.ds(t, GROUP, stride=per), :] = slot((2 + part) * per + t)
    for part in range(2):
        turned = KZ * pot[1 - part]
        w_new[part] = w[part] + (turned if part == 0 else -turned)
        copies[2 + part].start()
    row = lax.broadcasted_iota(jnp.int32, (rows, cols), 0)
    g = jnp.where((row == rows - 1) & (rank == steps - 1), 0.0, heavy[...])
    for part in range(2):
        here = pot[part]
        above = jnp.broadcast_to(edge[part : part + 1, :], (rows, cols))
        after = jnp.where(row == rows - 1, above, pltpu.roll(here, rows - 1, 0))
        v_new[part] = v[part] - g * (after - here)
        copies[4 + part].start()
    for copy in copies:
        copy.wait()


def call(body, outs, scratch, ins, out_spec=VMEM, semaphores=0, limit=24):
    scratch = [pltpu.VMEM(shape, F32) for shape in scratch]
    if semaphores:
        scratch.append(pltpu.SemaphoreType.DMA((semaphores,)))
    return pl.pallas_call(
        body,
        out_shape=[jax.ShapeDtypeStruct(shape, F32) for shape in outs],
        in_specs=ins,
        out_specs=[out_spec] * len(outs),
        scratch_shapes=scratch,
        compiler_params=pltpu.CompilerParams(vmem_limit_bytes=limit * 1024 * 1024),
        cost_estimate=pl.CostEstimate(flops=1000000, bytes_accessed=1000000, transcendentals=0),
    )


def exchange(array, axis, count, groups=None):
    shape = array.shape
    array = array.reshape(count, shape[0] // count * shape[1])
    return lax.all_to_all(array, axis, 0, 0, axis_index_groups=groups, tiled=True).reshape(shape)


def per_device(u_star, v_star, w_star, cell_width, face_weight):
    nodes, steps = lax.axis_size("gx"), lax.axis_size("gy")
    shape = u_star.shape
    rows, cols = shape[2:]
    wider = rows // GROUP
    across_f, across_i, across_full, along_f, along_i, along_full, turn_f, turn_i, waves = tables(nodes, cols)
    u, v, w = (x.reshape(2, rows, cols) for x in (u_star, v_star, w_star))
    field, plane, line = (2, rows, cols), (rows, cols), (1, rows)
    (near_out, all_out), (near_back, all_back) = (
        ([ranks[i : i + GROUP] for i in range(0, nodes, GROUP)], [ranks])
        for ranks in (order(nodes, OUT), order(nodes, BACK))
    )

    send, wide, heavy = call(
        prepare,
        [(GROUP * (4 * wider + 2), cols), plane, plane],
        [field, field, field, line, line, (4, rows, cols)],
        [HBM] * 5,
        semaphores=5,
    )(*(pltpu.with_memory_space_constraint(x, pltpu.HBM) for x in (u, v, w, cell_width.reshape(line), face_weight.reshape(line))))
    got = exchange(send, "gx", GROUP, near_out)
    (send,) = call(functools.partial(forward, nodes), [(nodes * (2 * wider + 1), cols)], [], [VMEM] * 4)(
        got, across_f, along_f, turn_f
    )
    got = exchange(send, "gx", nodes, all_out)
    base, left, right, tree, send = call(
        functools.partial(eliminate, nodes),
        [field, plane, plane, (LEVELS, 8, SEGMENTS, cols), (8 * steps, cols)],
        [field],
        [VMEM] * 3,
    )(got, wide, heavy)
    got = exchange(send, "gy", steps)
    (send,) = call(
        functools.partial(couple, nodes, steps), [(nodes * (2 * wider + 2), cols)], [(6, steps, cols)], [VMEM] * 5
    )(got, base, left, right, tree)
    got = exchange(send, "gx", nodes, all_back)
    send, edge = call(
        functools.partial(inverse, nodes), [(GROUP * 4 * wider, cols), (8, cols)], [(2 * GROUP, cols)], [VMEM] * 7
    )(got, across_i, across_full, along_i, along_full, turn_i, waves)
    got = exchange(send, "gx", GROUP, near_back)
    outs = call(
        functools.partial(finish, steps),
        [field] * 3,
        [field] * 4,
        [VMEM] * 6,
        out_spec=HBM,
        semaphores=6,
    )(u, v, w, got, edge, heavy)
    return tuple(x.reshape(shape) for x in outs)


def solution(mesh):
    whole = P(None, None, "gy", "gx")
    return jax.shard_map(
        per_device,
        mesh=mesh,
        in_specs=(whole, whole, whole, P("gy"), P("gy")),
        out_specs=(whole, whole, whole),
        check_vma=False,
    )
```
